32 devices in a mesh: dp: 2 (over core), seq: 4 (over y, x), expert: 4 (over z).
Axes of the slice: x: 2, y: 2, z: 4, core: 2. Of those that a mesh axis runs over, the one named last changes fastest.
Arguments:
- query_input: bfloat16 [8, 512, 1024], P(('dp', 'expert'), 'seq'), may hold values from -6 to 6
- key_input: bfloat16 [8, 512, 1024], P(('dp', 'expert'), 'seq'), may hold values from -6 to 6
- value_input: bfloat16 [8, 512, 1024], P(('dp', 'expert'), 'seq'), may hold values from -6 to 6
- routes: int32 [8, 512, 2], P(('dp', 'expert'), 'seq'), may hold values from 0 to 3, all different within a row; in each aligned block of 128 rows (0 to 127, 128 to 255, ..., all dimensions but the last counted through in order) at most 96 rows name the same one
- gate_values: float32 [8, 512, 2], P(('dp', 'expert'), 'seq'), may hold values from 0.2 to 1
- up_weight: bfloat16 [4, 1024, 2048], P('expert'), may hold values from -0.1875 to 0.1875
- down_weight: bfloat16 [4, 2048, 1024], P('expert'), may hold values from -0.125 to 0.125
- cotangent: bfloat16 [8, 512, 1024], P(('dp', 'expert'), 'seq'), may hold values from -6 to 6
Outputs:
- layer_output: bfloat16 [8, 512, 1024], P(('dp', 'expert'), 'seq')
- grad_queries: bfloat16 [8, 512, 1024], P(('dp', 'expert'), 'seq')
- grad_keys: bfloat16 [8, 512, 1024], P(('dp', 'expert'), 'seq')
- grad_values: bfloat16 [8, 512, 1024], P(('dp', 'expert'), 'seq')
- grad_up: float32 [4, 1024, 2048], P('expert', ('dp', 'seq'))
- grad_down: float32 [4, 2048, 1024], P('expert', None, ('dp', 'seq'))
The draws below stay inside these ranges and needn't reach their ends.
Inputs may be any that keep to these rules, and one draw needn't show every extreme that they name: `routes`: each token names 2 different experts. The 128 tokens of one device (aligned blocks of rows) name any one expert at most 96 times, and in every draw some device's tokens name some expert exactly 96 times.
All inputs are finite; a program needn't handle non-finite values.
Results may differ from the reference program's by a relative error of at most 0.017.
Values may be sent and summed in bfloat16 or wider, within the bound.
A program may use at most 128 MiB of HBM per device.

```python
import math
import jax
import jax.numpy as jnp
import numpy as np
from jax import lax

D = 1024
HEADS = 8
DH = 128
HID = 2048
TOP = 2
TOK_DEV = 128
L = 512
SEQS = 8
EXPERTS = 4
CAP = 96
N_SEQ = 4


def draw_query_input(key, part):
    normal_rows = jax.random.normal(jax.random.fold_in(key, 1), (SEQS, L, D), jnp.float32)
    return jnp.clip(1.5 * normal_rows, -6.0, 6.0).astype(jnp.bfloat16)


def draw_key_input(key, part):
    normal_rows = jax.random.normal(jax.random.fold_in(key, 5), (SEQS, L, D), jnp.float32)
    return jnp.clip(1.5 * normal_rows, -6.0, 6.0).astype(jnp.bfloat16)


def block_levels(own_key, extent, split, low, top_value):
    gain = 1.0
    for dim, shards_of in split:
        draws = jax.random.uniform(jax.random.fold_in(jax.random.fold_in(own_key, 6), dim), (shards_of,), jnp.float32, low / len(split), top_value / len(split))
        gain = gain * jnp.repeat(jnp.exp(draws), extent[dim] // shards_of).reshape((-1,) + (1,) * (len(extent) - 1 - dim))
    return gain


def assign_block(key, own, number, rows, number_of, top, bound, slope):
    order = jax.random.permutation(key, number_of)
    crowded, ordinary = shares(number_of, rows * top, bound, slope, True), shares(number_of, rows * top, bound, slope, False)
    places = jnp.arange(number_of)

    def named(sizes, rotation):
        used = int((sizes > 0).sum())
        fixed = max(1, used // 4)
        passed = fixed + (places - fixed + rotation * (used - fixed)) % max(1, number_of - fixed)
        return jnp.zeros((number_of,), jnp.int32).at[order[jnp.where(places < fixed, places, passed)]].set(jnp.asarray(sizes, jnp.int32))

    sizes = jnp.where(number % 4 == 0, named(crowded, number // 4), named(ordinary, number - number // 4 - 1))
    mixed = jax.random.permutation(jax.random.fold_in(own, 3), number_of)
    donor, sink = mixed[0:number_of // 2 * 2:2], mixed[1:number_of // 2 * 2:2]
    room = jnp.minimum(sizes[donor] - 1, bound - sizes[sink]) // 2
    room = jnp.where((donor == order[0]) | (sink == order[0]) | (sizes[sink] == 0), 0, jnp.maximum(room, 0))
    passed = jax.random.randint(jax.random.fold_in(own, 4), (number_of // 2,), 0, 1 << 20) % (room + 1)
    sizes = sizes.at[donor].add(-passed).at[sink].add(passed)
    members = jnp.searchsorted(jnp.cumsum(sizes), jnp.arange(rows * top), side="right").astype(jnp.int32)
    listing = members.reshape(top, rows).T
    listing = listing[jax.random.permutation(jax.random.fold_in(own, 1), rows)]
    rotation = jax.random.randint(jax.random.fold_in(own, 2), (rows, 1), 0, top)
    return jnp.take_along_axis(listing, (jnp.arange(top)[None, :] + rotation) % top, axis=1)


def shares(number_of, total, bound, lean, full):
    portions = [(1 << 20) // math.isqrt(grade ** lean) + 1 for grade in range(1, number_of + 1)]
    largest = bound if full else min(bound, max(-(-total // number_of), total * portions[0] // sum(portions)))
    least = 1 if total - largest >= number_of - 1 else 0
    holding, rest = [largest] + [least] * (number_of - 1), total - largest - least * (number_of - 1)
    while rest > 0:
        movable = [i for i in range(1, number_of) if holding[i] < largest] or [i for i in range(1, number_of) if holding[i] < bound]
        mass, remaining = sum([portions[i] for i in movable]), rest
        for i in movable:
            extra = min(bound - holding[i], max(1, remaining * portions[i] // mass), rest)
            holding[i] = holding[i] + extra
            rest = rest - extra
    return np.array(holding)


def scatter_about(own_key, dims, width, limit, shards=(), held_as=jnp.bfloat16):
    array = jax.random.normal(own_key, dims, jnp.float32) * width
    if len(shards) > 0:
        array = block_levels(own_key, dims, shards, -0.22, 0.18) * array
    return jnp.clip(array, min=-limit, max=limit).astype(held_as)


def setup_inputs(seed: int = 0) -> dict:
    keys = jax.random.split(jax.random.key(seed), 9)
    query_input = draw_query_input(jax.random.fold_in(keys[8], 71), 0)
    key_input = draw_key_input(jax.random.fold_in(keys[8], 71), 0)
    value_input = scatter_about(keys[2], (SEQS, L, D), 1.0, 6.0, ((0, 8), (1, 4)))
    routes_keys = jax.random.split(jax.random.fold_in(keys[3], 1), SEQS * L // TOK_DEV)
    routes_turns = jax.random.permutation(jax.random.fold_in(keys[3], 3), SEQS * L // TOK_DEV)
    routes = jax.vmap(lambda own, number: assign_block(jax.random.fold_in(keys[3], 2), own, number, TOK_DEV, EXPERTS, TOP, CAP, 2))(routes_keys, routes_turns).reshape((SEQS, L, TOP))
    gate_values = jnp.clip(0.2 + 0.8 * jax.random.uniform(keys[4], (SEQS, L, TOP), jnp.float32) ** block_levels(keys[4], (SEQS, L, TOP), ((0, 8), (1, 4)), -0.2, 0.2), 0.2, 1.0)
    up_weight = scatter_about(keys[5], (EXPERTS, D, HID), D ** -0.5, 0.1875, ((0, 4),))
    down_weight = scatter_about(keys[6], (EXPERTS, HID, D), HID ** -0.5, 0.125, ((0, 4),))
    cotangent = scatter_about(keys[7], (SEQS, L, D), 1.0, 6.0, ((0, 8), (1, 4)))
    return {"query_input": query_input, "key_input": key_input, "value_input": value_input, "routes": routes, "gate_values": gate_values, "up_weight": up_weight, "down_weight": down_weight, "cotangent": cotangent}


EPSILON = 1e-06
GELU_COEF = math.sqrt(2.0 / math.pi)

def gelu_pair(inputs):
    cubic = inputs + 0.044715 * inputs * inputs * inputs
    hyper = jnp.tanh(GELU_COEF * cubic)
    result = 0.5 * inputs * (1.0 + hyper)
    slope_value = 0.5 * (1.0 + hyper) + 0.5 * inputs * (1.0 - hyper * hyper) * GELU_COEF * (1.0 + 3.0 * 0.044715 * inputs * inputs)
    return (result, slope_value)

def prob_table(query_rows, key_rows):
    scaling = 1.0 / math.sqrt(DH)
    scores = jnp.einsum('qhd,khd->hqk', query_rows.astype(jnp.float32), key_rows.astype(jnp.float32)) * scaling
    highest = lax.optimization_barrier(jnp.max(scores, axis=-1, keepdims=True))
    exponent = jnp.exp(scores - highest)
    return exponent / lax.optimization_barrier(jnp.sum(exponent, axis=-1, keepdims=True))

def split_heads(tensor):
    return tensor.reshape(L, HEADS, DH)

def attend_forward(triple):
    query_rows = split_heads(triple[0])
    key_rows = split_heads(triple[1])
    value_rows = split_heads(triple[2])
    prob_rows = prob_table(query_rows, key_rows)
    prob_bf = prob_rows.astype(jnp.bfloat16)
    output = jnp.einsum('hqk,khd->qhd', prob_bf.astype(jnp.float32), value_rows.astype(jnp.float32))
    return output.astype(jnp.bfloat16).reshape(L, D)

def attend_backward(quad):
    query_rows = split_heads(quad[0])
    key_rows = split_heads(quad[1])
    value_rows = split_heads(quad[2])
    upstream = split_heads(quad[3])
    scaling = 1.0 / math.sqrt(DH)
    prob_rows = prob_table(query_rows, key_rows)
    prob_bf = prob_rows.astype(jnp.bfloat16)
    grad_probs = jnp.einsum('qhd,khd->hqk', upstream.astype(jnp.float32), value_rows.astype(jnp.float32))
    row_delta = lax.optimization_barrier(jnp.sum(prob_rows * grad_probs, axis=-1, keepdims=True))
    grad_scores = (prob_rows * (grad_probs - row_delta) * scaling).astype(jnp.bfloat16)
    grad_query = jnp.einsum('hqk,khd->qhd', grad_scores.astype(jnp.float32), key_rows.astype(jnp.float32))
    grad_key = jnp.einsum('hqk,qhd->khd', grad_scores.astype(jnp.float32), query_rows.astype(jnp.float32))
    grad_value = jnp.einsum('hqk,qhd->khd', prob_bf.astype(jnp.float32), upstream.astype(jnp.float32))
    return (grad_query.astype(jnp.bfloat16).reshape(L, D), grad_key.astype(jnp.bfloat16).reshape(L, D), grad_value.astype(jnp.bfloat16).reshape(L, D))

def reference(query_input, key_input, value_input, routes, gate_values, up_weight, down_weight, cotangent):
    attended = lax.map(attend_forward, (query_input, key_input, value_input))
    token_count = SEQS * L
    attended_f = attended.reshape(token_count, D).astype(jnp.float32)
    inverse_rms = lax.rsqrt(lax.optimization_barrier(jnp.mean(attended_f * attended_f, axis=-1, keepdims=True)) + EPSILON)
    unit_rows = attended_f * inverse_rms
    normed = unit_rows.astype(jnp.bfloat16)
    chosen = routes.reshape(-1).astype(jnp.int32)
    gate_rows = gate_values.reshape(token_count, TOP).astype(jnp.float32)
    upstream = cotangent.reshape(token_count, D).astype(jnp.float32)
    grad_out_rows = (gate_rows[:, :, None] * upstream[:, None, :]).astype(jnp.bfloat16).reshape(token_count * TOP, D)
    room_rows = SEQS * N_SEQ * CAP

    def per_expert(running, expert):
        out_acc, grad_acc = running
        picked = jnp.argsort((chosen != expert).astype(jnp.int32), stable=True)[:room_rows].astype(jnp.int32)
        live_mask = (chosen[picked] == expert)[:, None]
        rows_in = jnp.where(live_mask, normed[picked // TOP], jnp.zeros((), jnp.bfloat16))
        grads_in = jnp.where(live_mask, grad_out_rows[picked], jnp.zeros((), jnp.bfloat16))
        weight_in = up_weight[expert]
        weight_out = down_weight[expert]
        pre_act = jnp.dot(rows_in, weight_in, preferred_element_type=jnp.float32)
        act_value, act_slope = gelu_pair(pre_act)
        activated = act_value.astype(jnp.bfloat16)
        produced = jnp.dot(activated, weight_out, preferred_element_type=jnp.float32).astype(jnp.bfloat16)
        grad_act = jnp.dot(grads_in, weight_out.T, preferred_element_type=jnp.float32)
        grad_pre = (grad_act * act_slope).astype(jnp.bfloat16)
        grad_down_e = jnp.dot(activated.T, grads_in, preferred_element_type=jnp.float32)
        grad_up_e = jnp.dot(rows_in.T, grad_pre, preferred_element_type=jnp.float32)
        grad_normed = jnp.dot(grad_pre, weight_in.T, preferred_element_type=jnp.float32).astype(jnp.bfloat16)
        out_acc = out_acc.at[picked].add(jnp.where(live_mask, produced, jnp.zeros((), jnp.bfloat16)))
        grad_acc = grad_acc.at[picked].add(jnp.where(live_mask, grad_normed, jnp.zeros((), jnp.bfloat16)))
        return ((out_acc, grad_acc), (grad_up_e, grad_down_e))
    start_rows = jnp.zeros((token_count * TOP, D), jnp.bfloat16)
    (out_acc, grad_acc), (grad_up, grad_down) = lax.scan(per_expert, (start_rows, start_rows), jnp.arange(EXPERTS, dtype=jnp.int32))
    returned = out_acc.reshape(token_count, TOP, D).astype(jnp.float32)
    expert_mix = lax.optimization_barrier(jnp.sum(gate_rows[:, :, None] * returned, axis=1))
    layer_output = (attended_f + expert_mix).astype(jnp.bfloat16).reshape(SEQS, L, D)
    grad_unit = lax.optimization_barrier(jnp.sum(grad_acc.reshape(token_count, TOP, D).astype(jnp.float32), axis=1))
    grad_attended = upstream + inverse_rms * (grad_unit - unit_rows * lax.optimization_barrier(jnp.mean(grad_unit * unit_rows, axis=-1, keepdims=True)))
    grad_attended = grad_attended.astype(jnp.bfloat16).reshape(SEQS, L, D)
    grad_queries, grad_keys, grad_values = lax.map(attend_backward, (query_input, key_input, value_input, grad_attended))
    return (layer_output, grad_queries, grad_keys, grad_values, grad_up, grad_down)
```

```python
import functools
import math

import jax
import jax.numpy as jnp
from jax import lax
from jax.experimental import pallas as pl
from jax.experimental.pallas import tpu as pltpu
from jax.sharding import PartitionSpec as P

DH = 128
TOP = 2
EPSILON = 1e-06
GELU_COEF = math.sqrt(2.0 / math.pi)
MESH = pl.DeviceIdType.MESH
F32 = jnp.float32
BF16 = jnp.bfloat16
VMEM_LIMIT = 52 * 1024 * 1024


def gelu_pair(inputs):
    square = inputs * inputs
    hyper = jnp.tanh(GELU_COEF * inputs * (1.0 + 0.044715 * square))
    half = 0.5 * (1.0 + hyper)
    result = inputs * half
    slope = half + 0.5 * inputs * (1.0 - hyper * hyper) * GELU_COEF * (
        1.0 + 3.0 * 0.044715 * square
    )
    return result, slope


def dot_nn(a, b):
    return jnp.dot(a, b, preferred_element_type=F32)


def dot_nt(a, b):
    return lax.dot_general(a, b, (((1,), (1,)), ((), ())), preferred_element_type=F32)


def dot_tn(a, b):
    return lax.dot_general(a, b, (((0,), (0,)), ((), ())), preferred_element_type=F32)


def greet(axes):
    barrier = pltpu.get_barrier_semaphore()
    total = 0
    for axis in axes:
        size = lax.axis_size(axis)
        me = lax.axis_index(axis)
        for step in range(1, size):
            peer = lax.rem(me + step, size)
            pl.semaphore_signal(barrier, inc=1, device_id={axis: peer}, device_id_type=MESH)
            total += 1
    pl.semaphore_wait(barrier, total)


def remote(src, dst, send, recv, axis, peer):
    return pltpu.make_async_remote_copy(
        src_ref=src,
        dst_ref=dst,
        send_sem=send,
        recv_sem=recv,
        device_id={axis: peer},
        device_id_type=MESH,
    )


def split_cols(src, dst, send, recv, me, size):
    rows = src.shape[0]
    width = src.shape[1] // size
    copies = []
    for step in range(1, size):
        peer = lax.rem(me + step, size)
        copy = remote(
            src.at[:, pl.ds(pl.multiple_of(peer * width, width), width)],
            dst.at[pl.ds(pl.multiple_of(me * rows, rows), rows), :],
            send.at[step],
            recv.at[step],
            "seq",
            peer,
        )
        copy.start()
        copies.append(copy)
    own = src[:, pl.ds(pl.multiple_of(me * width, width), width)]
    dst[pl.ds(pl.multiple_of(me * rows, rows), rows), :] = own
    return copies


def join_block(src, dst, send, recv, me, size, step):
    rows = dst.shape[0]
    width = src.shape[1]
    peer = lax.rem(me + step, size)
    copy = remote(
        src.at[pl.ds(pl.multiple_of(peer * rows, rows), rows), :],
        dst.at[:, pl.ds(pl.multiple_of(me * width, width), width)],
        send.at[step],
        recv.at[step],
        "seq",
        peer,
    )
    copy.start()
    return copy


def join_rows(src, dst, send, recv, me, size):
    rows = dst.shape[0]
    width = src.shape[1]
    copies = [join_block(src, dst, send, recv, me, size, step) for step in range(1, size)]
    own = src[pl.ds(pl.multiple_of(me * rows, rows), rows), :]
    dst[:, pl.ds(pl.multiple_of(me * width, width), width)] = own
    return copies


def swap_slots(src, dst, send, recv, me, size):
    cap = src.shape[0] // size
    copies = []
    for step in range(1, size):
        peer = lax.rem(me + step, size)
        copy = remote(
            src.at[pl.ds(pl.multiple_of(peer * cap, cap), cap), :],
            dst.at[pl.ds(pl.multiple_of(me * cap, cap), cap), :],
            send.at[step],
            recv.at[step],
            "expert",
            peer,
        )
        copy.start()
        copies.append(copy)
    mine = pl.ds(pl.multiple_of(me * cap, cap), cap)
    dst[mine, :] = src[mine, :]
    return copies


def wait_all(copies):
    for copy in copies:
        copy.wait()


def softmax_rows(query, key):
    scores = dot_nt(query, key) * (1.0 / math.sqrt(DH))
    exponent = jnp.exp(scores - jnp.max(scores, axis=-1, keepdims=True))
    return exponent / jnp.sum(exponent, axis=-1, keepdims=True)


def forward_kernel(
    experts, cap,
    q_ref, k_ref, v_ref, routes_ref, gates_ref, cot_ref,
    qh_ref, kh_ref, vh_ref, att_ref, place_ref, grad_ref,
    packed, heads, seq_send, seq_recv, exp_send, exp_recv,
):
    n_seq = lax.axis_size("seq")
    n_exp = lax.axis_size("expert")
    me_seq = lax.axis_index("seq")
    me_exp = lax.axis_index("expert")
    rows = q_ref.shape[0]
    slots = experts * cap
    greet(("seq", "expert"))
    seq_copies = []
    for number, (src, dst) in enumerate(((q_ref, qh_ref), (k_ref, kh_ref), (v_ref, vh_ref))):
        seq_copies += split_cols(
            src, dst, seq_send.at[number], seq_recv.at[number], me_seq, n_seq
        )

    expert_ids = lax.broadcasted_iota(jnp.int32, (rows, experts), 1)
    hits = [
        jnp.where(routes_ref[:, j : j + 1] == expert_ids, 1.0, 0.0).astype(F32)
        for j in range(TOP)
    ]
    earlier = lax.broadcasted_iota(jnp.int32, (rows, rows), 1) < lax.broadcasted_iota(
        jnp.int32, (rows, rows), 0
    )
    rank = dot_nn(
        jnp.where(earlier, 1.0, 0.0).astype(BF16), (hits[0] + hits[1]).astype(BF16)
    )
    base = rank + (expert_ids * cap).astype(F32)
    slot_ids = lax.broadcasted_iota(jnp.int32, (rows, slots), 1).astype(F32)
    cot = cot_ref[...].astype(F32)
    total = None
    for j in range(TOP):
        slot = jnp.sum(hits[j] * base, axis=1, keepdims=True)
        placer = jnp.where(slot_ids == slot, 1.0, 0.0).astype(BF16)
        place_ref[j] = placer
        dout = (gates_ref[:, j : j + 1] * cot).astype(BF16)
        part = dot_tn(placer, dout)
        total = part if total is None else total + part
    packed[...] = total.astype(BF16)
    exp_copies = swap_slots(packed, grad_ref, exp_send, exp_recv, me_exp, n_exp)

    wait_all(seq_copies)
    width = heads.shape[1]
    back = []
    for step in [*range(1, n_seq), 0]:
        peer = lax.rem(me_seq + step, n_seq)
        block = pl.ds(pl.multiple_of(peer * rows, rows), rows)
        for head in range(width // DH):
            cols = slice(head * DH, (head + 1) * DH)
            probs = softmax_rows(qh_ref[block, cols], kh_ref[:, cols]).astype(BF16)
            heads[block, cols] = dot_nn(probs, vh_ref[:, cols]).astype(BF16)
        if step > 0:
            back.append(
                join_block(heads, att_ref, seq_send.at[3], seq_recv.at[3], me_seq, n_seq, step)
            )
        else:
            att_ref[:, pl.ds(pl.multiple_of(me_seq * width, width), width)] = heads[block, :]
    wait_all(back)
    wait_all(exp_copies)


def unit_of(att):
    att_f = att.astype(F32)
    inverse = lax.rsqrt(jnp.mean(att_f * att_f, axis=-1, keepdims=True) + EPSILON)
    return att_f, inverse, att_f * inverse


def expert_kernel(
    chunk,
    att_ref, place_ref, grad_ref, up_hbm, down_hbm,
    out_ref, dnorm_ref, gw_ref,
    packed, rows_in, up, down, dact, act, dpre, rows_t, grad_t,
    exp_send, exp_recv, load_sem,
):
    n_exp = lax.axis_size("expert")
    me_exp = lax.axis_index("expert")
    load_up = pltpu.make_async_copy(up_hbm, up, load_sem.at[0])
    load_down = pltpu.make_async_copy(down_hbm, down, load_sem.at[1])
    load_down.start()
    load_up.start()
    _, _, unit = unit_of(att_ref[...])
    placer = place_ref[0] + place_ref[1]
    packed[...] = dot_tn(placer, unit.astype(BF16)).astype(BF16)
    greet(("expert",))
    copies = swap_slots(packed, rows_in, exp_send, exp_recv, me_exp, n_exp)
    grad_t[...] = grad_ref[...].T
    load_down.wait()
    hidden = up.shape[1]
    model = up.shape[0]

    @pl.loop(0, hidden // chunk)
    def _(c):
        cols = pl.ds(pl.multiple_of(c * chunk, chunk), chunk)
        dact[:, cols] = dot_nt(grad_ref[...], down[cols, :])

    load_up.wait()
    wait_all(copies)

    @pl.loop(0, hidden // chunk)
    def _(c):
        cols = pl.ds(pl.multiple_of(c * chunk, chunk), chunk)
        value, slope = gelu_pair(dot_nn(rows_in[...], up[:, cols]))
        act[:, cols] = value.astype(BF16)
        dpre[:, cols] = (dact[:, cols] * slope).astype(BF16)

    @pl.loop(0, model // 256)
    def _(c):
        cols = pl.ds(pl.multiple_of(c * 256, 256), 256)
        dnorm_ref[:, cols] = dot_nt(dpre[...], up[cols, :]).astype(BF16)
        out_ref[:, cols] = dot_nn(act[...], down[:, cols]).astype(BF16)

    rows_t[...] = rows_in[...].T

    @pl.loop(0, hidden // chunk)
    def _(c):
        cols = pl.ds(pl.multiple_of(c * chunk, chunk), chunk)
        later = pl.ds(pl.multiple_of(hidden + c * chunk, chunk), chunk)
        gw_ref[:, cols] = dot_nn(rows_t[...], dpre[:, cols]).astype(BF16)
        gw_ref[:, later] = dot_nn(grad_t[...], act[:, cols]).astype(BF16)


def backward_kernel(
    out_ref, dnorm_ref, place_ref, gates_ref, cot_ref, att_ref, qh_ref, kh_ref, vh_ref,
    layer_ref, gq_ref, gk_ref, gv_ref,
    ret_out, ret_dnorm, datt, dheads, probs, gqh, gkh, gvh,
    seq_send, seq_recv, exp_send, exp_recv,
):
    n_seq = lax.axis_size("seq")
    n_exp = lax.axis_size("expert")
    me_seq = lax.axis_index("seq")
    me_exp = lax.axis_index("expert")
    greet(("seq", "expert"))
    dnorm_copies = swap_slots(
        dnorm_ref, ret_dnorm, exp_send.at[0], exp_recv.at[0], me_exp, n_exp
    )
    out_copies = swap_slots(out_ref, ret_out, exp_send.at[1], exp_recv.at[1], me_exp, n_exp)
    width = qh_ref.shape[1]
    for head in range(width // DH):
        cols = slice(head * DH, (head + 1) * DH)
        probs[head] = softmax_rows(qh_ref[:, cols], kh_ref[:, cols])
    att_f, inverse, unit = unit_of(att_ref[...])
    cot = cot_ref[...].astype(F32)
    wait_all(dnorm_copies)
    dunit = dot_nn(place_ref[0] + place_ref[1], ret_dnorm[...])
    datt[...] = (
        cot + inverse * (dunit - unit * jnp.mean(dunit * unit, axis=-1, keepdims=True))
    ).astype(BF16)
    wait_all(split_cols(datt, dheads, seq_send.at[0], seq_recv.at[0], me_seq, n_seq))
    scaling = 1.0 / math.sqrt(DH)
    for head in range(width // DH):
        cols = slice(head * DH, (head + 1) * DH)
        prob = probs[head]
        dhead = dheads[:, cols]
        gvh[:, cols] = dot_tn(prob.astype(BF16), dhead).astype(BF16)
        dprobs = dot_nt(dhead, vh_ref[:, cols])
        delta = jnp.sum(prob * dprobs, axis=-1, keepdims=True)
        dscores = (prob * (dprobs - delta) * scaling).astype(BF16)
        gkh[:, cols] = dot_tn(dscores, qh_ref[:, cols]).astype(BF16)
        gqh[:, cols] = dot_nn(dscores, kh_ref[:, cols]).astype(BF16)
    back = []
    for number, (src, dst) in enumerate(((gvh, gv_ref), (gkh, gk_ref), (gqh, gq_ref)), 1):
        back += join_rows(src, dst, seq_send.at[number], seq_recv.at[number], me_seq, n_seq)
    wait_all(out_copies)
    mixed = att_f
    mix = None
    for j in range(TOP):
        part = gates_ref[:, j : j + 1] * dot_nn(place_ref[j], ret_out[...])
        mix = part if mix is None else mix + part
    layer_ref[...] = (mixed + mix).astype(BF16)
    wait_all(back)


def shards(
    query_input, key_input, value_input, routes, gate_values, up_weight, down_weight, cotangent
):
    rows, model = query_input.shape[1:]
    n_seq = lax.axis_size("seq")
    n_exp = lax.axis_size("expert")
    hidden = up_weight.shape[2]
    experts = up_weight.shape[0] * n_exp
    cap = rows * TOP * 3 // (2 * experts)
    cap = -(-cap // 16) * 16
    slots = experts * cap
    width = model // n_seq
    tokens = rows * n_seq
    vmem = pl.BlockSpec(memory_space=pltpu.VMEM)
    hbm = pl.BlockSpec(memory_space=pl.ANY)
    dma = pltpu.SemaphoreType.DMA

    def shape(*dims, dtype=BF16):
        return jax.ShapeDtypeStruct(dims, dtype)

    def params(number):
        return pltpu.CompilerParams(
            collective_id=number, has_side_effects=True, vmem_limit_bytes=VMEM_LIMIT
        )

    gates = gate_values[0]
    cot = cotangent[0]
    qh, kh, vh, attended, placers, grad_in = pl.pallas_call(
        functools.partial(forward_kernel, experts, cap),
        name="attention_forward",
        out_shape=[shape(tokens, width)] * 3
        + [shape(rows, model), shape(TOP, rows, slots), shape(slots, model)],
        in_specs=[vmem] * 6,
        out_specs=[vmem] * 6,
        scratch_shapes=[
            pltpu.VMEM((slots, model), BF16),
            pltpu.VMEM((tokens, width), BF16),
            dma((4, n_seq)),
            dma((4, n_seq)),
            dma((n_exp,)),
            dma((n_exp,)),
        ],
        compiler_params=params(0),
        cost_estimate=pl.CostEstimate(
            flops=4 * tokens * tokens * width, bytes_accessed=8 * rows * model,
            transcendentals=0,
        ),
    )(query_input[0], key_input[0], value_input[0], routes[0], gates, cot)
    produced, dnormed, weight_grads = pl.pallas_call(
        functools.partial(expert_kernel, 512),
        name="expert_block",
        out_shape=[shape(slots, model), shape(slots, model), shape(model, 2 * hidden)],
        in_specs=[vmem] * 3 + [hbm] * 2,
        out_specs=[vmem] * 3,
        scratch_shapes=[
            pltpu.VMEM((slots, model), BF16),
            pltpu.VMEM((slots, model), BF16),
            pltpu.VMEM((model, hidden), BF16),
            pltpu.VMEM((hidden, model), BF16),
            pltpu.VMEM((slots, hidden), F32),
            pltpu.VMEM((slots, hidden), BF16),
            pltpu.VMEM((slots, hidden), BF16),
            pltpu.VMEM((model, slots), BF16),
            pltpu.VMEM((model, slots), BF16),
            dma((n_exp,)),
            dma((n_exp,)),
            dma((2,)),
        ],
        compiler_params=params(1),
        cost_estimate=pl.CostEstimate(
            flops=12 * slots * model * hidden, bytes_accessed=8 * model * hidden,
            transcendentals=0,
        ),
    )(attended, placers, grad_in, up_weight[0], down_weight[0])
    halves = lax.psum_scatter(weight_grads, "dp", scatter_dimension=0, tiled=True)
    summed = lax.psum_scatter(halves, "seq", scatter_dimension=0, tiled=True)
    layer, grad_q, grad_k, grad_v = pl.pallas_call(
        backward_kernel,
        name="attention_backward",
        out_shape=[shape(rows, model)] * 4,
        in_specs=[vmem] * 9,
        out_specs=[vmem] * 4,
        scratch_shapes=[
            pltpu.VMEM((slots, model), BF16),
            pltpu.VMEM((slots, model), BF16),
            pltpu.VMEM((rows, model), BF16),
            pltpu.VMEM((tokens, width), BF16),
            pltpu.VMEM((width // DH, tokens, tokens), F32),
            pltpu.VMEM((tokens, width), BF16),
            pltpu.VMEM((tokens, width), BF16),
            pltpu.VMEM((tokens, width), BF16),
            dma((4, n_seq)),
            dma((4, n_seq)),
            dma((2, n_exp)),
            dma((2, n_exp)),
        ],
        compiler_params=params(2),
        cost_estimate=pl.CostEstimate(
            flops=60_000_000_000, bytes_accessed=100_000_000, transcendentals=0
        ),
    )(produced, dnormed, placers, gates, cot, attended, qh, kh, vh)
    summed = summed.astype(F32)
    return (
        layer[None],
        grad_q[None],
        grad_k[None],
        grad_v[None],
        summed[None, :, :hidden],
        summed[:, hidden:].T[None],
    )


def solution(mesh):
    tokens = P(("dp", "expert"), "seq", None)
    weights = P("expert", None, None)
    in_specs = (tokens,) * 5 + (weights, weights, tokens)
    out_specs = (tokens,) * 4 + (P("expert", ("dp", "seq"), None), P("expert", None, ("dp", "seq")))
    return jax.shard_map(shards, mesh=mesh, in_specs=in_specs, out_specs=out_specs, check_vma=False)
```

```python
import functools
import math

import jax
import jax.numpy as jnp
from jax import lax
from jax.experimental import pallas as pl
from jax.experimental.pallas import tpu as pltpu
from jax.sharding import PartitionSpec as P

DH = 128
TOP = 2
EPSILON = 1e-06
GELU_COEF = math.sqrt(2.0 / math.pi)
MESH = pl.DeviceIdType.MESH
F32 = jnp.float32
BF16 = jnp.bfloat16
VMEM_LIMIT = 60 * 1024 * 1024


def gelu_pair(inputs):
    square = inputs * inputs
    hyper = jnp.tanh(GELU_COEF * inputs * (1.0 + 0.044715 * square))
    half = 0.5 * (1.0 + hyper)
    result = inputs * half
    slope = half + 0.5 * inputs * (1.0 - hyper * hyper) * GELU_COEF * (
        1.0 + 3.0 * 0.044715 * square
    )
    return result, slope


def dot_nn(a, b):
    return jnp.dot(a, b, preferred_element_type=F32)


def dot_nt(a, b):
    return lax.dot_general(a, b, (((1,), (1,)), ((), ())), preferred_element_type=F32)


def dot_tn(a, b):
    return lax.dot_general(a, b, (((0,), (0,)), ((), ())), preferred_element_type=F32)


def greet(axes):
    barrier = pltpu.get_barrier_semaphore()
    total = 0
    for axis in axes:
        size = lax.axis_size(axis)
        me = lax.axis_index(axis)
        for step in range(1, size):
            peer = lax.rem(me + step, size)
            pl.semaphore_signal(barrier, inc=1, device_id={axis: peer}, device_id_type=MESH)
            total += 1
    pl.semaphore_wait(barrier, total)


def remote(src, dst, send, recv, axis, peer):
    return pltpu.make_async_remote_copy(
        src_ref=src,
        dst_ref=dst,
        send_sem=send,
        recv_sem=recv,
        device_id={axis: peer},
        device_id_type=MESH,
    )


def rows_of(index, count):
    return pl.ds(pl.multiple_of(index * count, count), count)


def split_cols(src, dst, send, recv, me, size, own_sem):
    rows = src.shape[0]
    width = src.shape[1] // size
    copies = []
    for step in range(1, size):
        peer = lax.rem(me + step, size)
        copy = remote(
            src.at[:, rows_of(peer, width)],
            dst.at[rows_of(me, rows), :],
            send.at[step],
            recv.at[step],
            "seq",
            peer,
        )
        copy.start()
        copies.append(copy)
    own = pltpu.make_async_copy(src.at[:, rows_of(me, width)], dst.at[rows_of(me, rows), :], own_sem)
    own.start()
    return copies, own


def join_block(src, dst, send, recv, me, size, step):
    rows = dst.shape[0]
    width = src.shape[1]
    peer = lax.rem(me + step, size)
    copy = remote(
        src.at[rows_of(peer, rows), :],
        dst.at[:, rows_of(me, width)],
        send.at[step],
        recv.at[step],
        "seq",
        peer,
    )
    copy.start()
    return copy


def join_rows(src, dst, send, recv, me, size):
    rows = dst.shape[0]
    width = src.shape[1]
    copies = [join_block(src, dst, send, recv, me, size, step) for step in range(1, size)]
    dst[:, rows_of(me, width)] = src[rows_of(me, rows), :]
    return copies


def swap_slots(src, dst, send, recv, me, size):
    cap = src.shape[0] // size
    copies = []
    for step in range(1, size):
        peer = lax.rem(me + step, size)
        copy = remote(
            src.at[rows_of(peer, cap), :],
            dst.at[rows_of(me, cap), :],
            send.at[step],
            recv.at[step],
            "expert",
            peer,
        )
        copy.start()
        copies.append(copy)
    dst[rows_of(me, cap), :] = src[rows_of(me, cap), :]
    return copies


def arrive(copies):
    for copy in copies:
        copy.wait_recv()


def softmax_rows(query, key):
    scores = dot_nt(query, key) * (1.0 / math.sqrt(DH))
    exponent = jnp.exp(scores - jnp.max(scores, axis=-1, keepdims=True))
    return exponent / jnp.sum(exponent, axis=-1, keepdims=True)


def as_column(row):
    size = row.shape[1]
    same = lax.broadcasted_iota(jnp.int32, (size, size), 0) == lax.broadcasted_iota(
        jnp.int32, (size, size), 1
    )
    return jnp.sum(jnp.where(same, row, 0.0), axis=1, keepdims=True)


def layer_kernel(
    experts, cap, chunk,
    q_hbm, k_hbm, v_hbm, routes_ref, gates_ref, up_hbm, down_hbm, cot_ref,
    layer_ref, gq_ref, gk_ref, gv_ref, gup_ref, gdown_ref,
    qh, kh, vh, heads, att, probs, datt, dheads, gqh, gkh, gvh,
    place, sent_grad, grad_in, sent_rows, rows_in, out_rows, dnorm_rows, ret_out, ret_dnorm,
    up, down, dact, act, dpre, rows_t, grad_t,
    gw_own, gw_other, gw_recv, a1_recv, b1_recv, a2_sent, a2_recv, b2_sent, b2_recv,
    seq_send, seq_recv, exp_send, exp_recv, dp_send, dp_recv, red_send, red_recv, local_sem,
):
    n_seq = lax.axis_size("seq")
    n_exp = lax.axis_size("expert")
    me_seq = lax.axis_index("seq")
    me_exp = lax.axis_index("expert")
    me_dp = lax.axis_index("dp")
    rows = cot_ref.shape[0]
    slots = experts * cap
    model, hidden = up.shape
    width = heads.shape[1]
    n_heads = width // DH
    sent = []

    load_down = pltpu.make_async_copy(down_hbm, down, local_sem.at[0])
    load_up = pltpu.make_async_copy(up_hbm, up, local_sem.at[1])
    greet(("seq", "expert", "dp"))

    seq_copies = []
    own_copies = []
    for number, (src, dst) in enumerate(((q_hbm, qh), (k_hbm, kh), (v_hbm, vh))):
        copies, own = split_cols(
            src, dst, seq_send.at[number], seq_recv.at[number], me_seq, n_seq,
            local_sem.at[2 + number],
        )
        seq_copies += copies
        own_copies.append(own)
    load_down.start()
    load_up.start()

    expert_ids = lax.broadcasted_iota(jnp.int32, (experts, rows), 0)
    hits = [
        jnp.where(routes_ref[j : j + 1, :] == expert_ids, 1.0, 0.0).astype(F32)
        for j in range(TOP)
    ]
    earlier = lax.broadcasted_iota(jnp.int32, (rows, rows), 0) < lax.broadcasted_iota(
        jnp.int32, (rows, rows), 1
    )
    rank = dot_nn(
        (hits[0] + hits[1]).astype(BF16), jnp.where(earlier, 1.0, 0.0).astype(BF16)
    )
    base = rank + (expert_ids * cap).astype(F32)
    slot_ids = lax.broadcasted_iota(jnp.int32, (slots, rows), 0).astype(F32)
    cot = cot_ref[...].astype(F32)
    gates = [as_column(gates_ref[j : j + 1, :]) for j in range(TOP)]
    packed = None
    for j in range(TOP):
        slot = jnp.sum(hits[j] * base, axis=0, keepdims=True)
        place[j] = jnp.where(slot_ids == slot, 1.0, 0.0).astype(BF16)
        part = dot_nn(place[j], (gates[j] * cot).astype(BF16))
        packed = part if packed is None else packed + part
    sent_grad[...] = packed.astype(BF16)
    grad_copies = swap_slots(sent_grad, grad_in, exp_send.at[0], exp_recv.at[0], me_exp, n_exp)
    sent += seq_copies + grad_copies

    for own in own_copies:
        own.wait()
    arrive(seq_copies)
    back = []
    for step in [*range(1, n_seq), 0]:
        block = rows_of(lax.rem(me_seq + step, n_seq), rows)
        for head in range(n_heads):
            cols = slice(head * DH, (head + 1) * DH)
            prob = softmax_rows(qh[block, cols], kh[:, cols])
            probs[head, block, :] = prob
            heads[block, cols] = dot_nn(prob.astype(BF16), vh[:, cols]).astype(BF16)
        if step > 0:
            back.append(
                join_block(heads, att, seq_send.at[3], seq_recv.at[3], me_seq, n_seq, step)
            )
        else:
            att[:, rows_of(me_seq, width)] = heads[block, :]
    arrive(back)
    sent += back

    att_f = att[...].astype(F32)
    inverse = lax.rsqrt(jnp.mean(att_f * att_f, axis=-1, keepdims=True) + EPSILON)
    placer = place[0] + place[1]
    sent_rows[...] = dot_nn(placer, (att_f * inverse).astype(BF16)).astype(BF16)
    row_copies = swap_slots(sent_rows, rows_in, exp_send.at[1], exp_recv.at[1], me_exp, n_exp)
    sent += row_copies
    arrive(grad_copies)
    load_down.wait()
    load_up.wait()

    @pl.loop(0, hidden // chunk)
    def _(c):
        cols = rows_of(c, chunk)
        dact[:, cols] = dot_nt(grad_in[...], down[cols, :])

    grad_t[...] = grad_in[...].T
    arrive(row_copies)

    @pl.loop(0, hidden // chunk)
    def _(c):
        cols = rows_of(c, chunk)
        value, slope = gelu_pair(dot_nn(rows_in[...], up[:, cols]))
        act[:, cols] = value.astype(BF16)
        dpre[:, cols] = (dact[:, cols] * slope).astype(BF16)

    @pl.loop(0, model // 256)
    def _(c):
        cols = rows_of(c, 256)
        dnorm_rows[:, cols] = dot_nt(dpre[...], up[cols, :]).astype(BF16)

    dnorm_copies = swap_slots(
        dnorm_rows, ret_dnorm, exp_send.at[2], exp_recv.at[2], me_exp, n_exp
    )
    sent += dnorm_copies

    rows_t[...] = rows_in[...].T
    half = model // 2
    part_rows = half // 2
    dp_copies = []

    def weight_grads(dst, start, base_row):
        @pl.loop(0, hidden // chunk)
        def _(c):
            cols = rows_of(c, chunk)
            later = pl.ds(pl.multiple_of(hidden + c * chunk, chunk), chunk)
            lines = pl.ds(pl.multiple_of(base_row + start, part_rows), part_rows)
            here = slice(start, start + part_rows)
            dst[here, cols] = dot_nn(rows_t[lines, :], dpre[:, cols]).astype(BF16)
            dst[here, later] = dot_nn(grad_t[lines, :], act[:, cols]).astype(BF16)

    for number in range(2):
        start = number * part_rows
        weight_grads(gw_other, start, (1 - me_dp) * half)
        copy = remote(
            gw_other.at[start : start + part_rows, :],
            gw_recv.at[start : start + part_rows, :],
            dp_send.at[number],
            dp_recv.at[number],
            "dp",
            1 - me_dp,
        )
        copy.start()
        dp_copies.append(copy)
    sent += dp_copies
    for number in range(2):
        weight_grads(gw_own, number * part_rows, me_dp * half)

    low = lax.rem(me_seq, 2)
    high = me_seq // 2
    peer_low = 2 * high + 1 - low
    peer_high = 2 * (1 - high) + low
    piece = half // n_seq
    first = slice(0, hidden)
    second = slice(hidden, 2 * hidden)

    def reduce_send(src, dst, number, peer):
        copy = remote(src, dst, red_send.at[number], red_recv.at[number], "seq", peer)
        copy.start()
        sent.append(copy)
        return copy

    a1, b1 = [], []
    for number in range(2):
        dp_copies[number].wait_recv()

        @pl.loop(0, 2 * hidden // chunk)
        def _(c):
            cols = rows_of(c, chunk)
            here = slice(number * part_rows, (number + 1) * part_rows)
            gw_own[here, cols] = (
                gw_own[here, cols].astype(F32) + gw_recv[here, cols].astype(F32)
            ).astype(BF16)

        a1.append(
            reduce_send(
                gw_own.at[rows_of(2 * number + 1 - low, piece), first],
                a1_recv.at[number], number, peer_low,
            )
        )
    for number in range(2):
        b1.append(
            reduce_send(
                gw_own.at[rows_of(2 * (1 - high) + number, piece), second],
                b1_recv.at[number], 2 + number, peer_high,
            )
        )

    @pl.loop(0, model // 256)
    def _(c):
        cols = rows_of(c, 256)
        out_rows[:, cols] = dot_nn(act[...], down[:, cols]).astype(BF16)

    out_copies = swap_slots(out_rows, ret_out, exp_send.at[3], exp_recv.at[3], me_exp, n_exp)
    sent += out_copies

    arrive(dnorm_copies)
    dunit = dot_tn(place[0] + place[1], ret_dnorm[...])
    att_f = att[...].astype(F32)
    inverse = lax.rsqrt(jnp.mean(att_f * att_f, axis=-1, keepdims=True) + EPSILON)
    unit = att_f * inverse
    datt[...] = (
        cot_ref[...].astype(F32)
        + inverse * (dunit - unit * jnp.mean(dunit * unit, axis=-1, keepdims=True))
    ).astype(BF16)
    datt_copies, own = split_cols(
        datt, dheads, seq_send.at[4], seq_recv.at[4], me_seq, n_seq, local_sem.at[5]
    )
    sent += datt_copies
    own.wait()
    arrive(datt_copies)

    scaling = 1.0 / math.sqrt(DH)
    for head in range(n_heads):
        cols = slice(head * DH, (head + 1) * DH)
        prob = probs[head]
        dhead = dheads[:, cols]
        gvh[:, cols] = dot_tn(prob.astype(BF16), dhead).astype(BF16)
        dprobs = dot_nt(dhead, vh[:, cols])
        delta = jnp.sum(prob * dprobs, axis=-1, keepdims=True)
        dscores = (prob * (dprobs - delta) * scaling).astype(BF16)
        gkh[:, cols] = dot_tn(dscores, qh[:, cols]).astype(BF16)
        gqh[:, cols] = dot_nn(dscores, kh[:, cols]).astype(BF16)
    last = []
    for number, (src, dst) in enumerate(((gvh, gv_ref), (gkh, gk_ref), (gqh, gq_ref)), 5):
        last += join_rows(src, dst, seq_send.at[number], seq_recv.at[number], me_seq, n_seq)
    sent += last

    arrive(a1)
    a2_sent[...] = (
        gw_own[rows_of(2 * (1 - high) + low, piece), first].astype(F32)
        + a1_recv[1 - high].astype(F32)
    ).astype(BF16)
    a2 = reduce_send(a2_sent, a2_recv, 4, peer_high)
    arrive(b1)
    b2_sent[...] = (
        gw_own[rows_of(2 * high + 1 - low, piece), second].astype(F32)
        + b1_recv[1 - low].astype(F32)
    ).astype(BF16)
    b2 = reduce_send(b2_sent, b2_recv, 5, peer_low)

    arrive(out_copies)
    mix = None
    for j in range(TOP):
        part = as_column(gates_ref[j : j + 1, :]) * dot_tn(place[j], ret_out[...])
        mix = part if mix is None else mix + part
    layer_ref[...] = (att[...].astype(F32) + mix).astype(BF16)

    mine = rows_of(me_seq, piece)
    a2.wait_recv()
    gup_ref[...] = (
        gw_own[mine, first].astype(F32) + a1_recv[high].astype(F32) + a2_recv[...].astype(F32)
    )
    b2.wait_recv()
    gdown_ref[...] = (
        gw_own[mine, second].astype(F32) + b1_recv[low].astype(F32) + b2_recv[...].astype(F32)
    ).T
    arrive(last)
    for copy in sent:
        copy.wait_send()


def shards(
    query_input, key_input, value_input, routes, gate_values, up_weight, down_weight, cotangent
):
    rows, model = query_input.shape[1:]
    n_seq = lax.axis_size("seq")
    n_exp = lax.axis_size("expert")
    hidden = up_weight.shape[2]
    experts = up_weight.shape[0] * n_exp
    cap = rows * TOP * 3 // (2 * experts)
    cap = -(-cap // 16) * 16
    slots = experts * cap
    width = model // n_seq
    tokens = rows * n_seq
    half = model // 2
    piece = half // n_seq
    vmem = pl.BlockSpec(memory_space=pltpu.VMEM)
    hbm = pl.BlockSpec(memory_space=pl.ANY)
    dma = pltpu.SemaphoreType.DMA

    def shape(*dims, dtype=BF16):
        return jax.ShapeDtypeStruct(dims, dtype)

    def buf(*dims, dtype=BF16):
        return pltpu.VMEM(dims, dtype)

    head_block = buf(tokens, width)
    slot_block = buf(slots, model)
    layer, grad_q, grad_k, grad_v, grad_up, grad_down = pl.pallas_call(
        functools.partial(layer_kernel, experts, cap, 512),
        name="layer",
        out_shape=[shape(rows, model)] * 4
        + [shape(piece, hidden, dtype=F32), shape(hidden, piece, dtype=F32)],
        in_specs=[hbm] * 3 + [vmem] * 2 + [hbm] * 2 + [vmem],
        out_specs=[vmem] * 6,
        scratch_shapes=[
            head_block, head_block, head_block, head_block,
            buf(rows, model),
            buf(width // DH, tokens, tokens, dtype=F32),
            buf(rows, model),
            head_block, head_block, head_block, head_block,
            buf(TOP, slots, rows),
            slot_block, slot_block, slot_block, slot_block,
            slot_block, slot_block, slot_block, slot_block,
            buf(model, hidden),
            buf(hidden, model),
            buf(slots, hidden, dtype=F32),
            buf(slots, hidden),
            buf(slots, hidden),
            buf(model, slots),
            buf(model, slots),
            buf(half, 2 * hidden),
            buf(half, 2 * hidden),
            buf(half, 2 * hidden),
            buf(2, piece, hidden),
            buf(2, piece, hidden),
            buf(piece, hidden), buf(piece, hidden), buf(piece, hidden), buf(piece, hidden),
            dma((8, n_seq)),
            dma((8, n_seq)),
            dma((4, n_exp)),
            dma((4, n_exp)),
            dma((2,)),
            dma((2,)),
            dma((6,)),
            dma((6,)),
            dma((6,)),
        ],
        compiler_params=pltpu.CompilerParams(
            collective_id=0, has_side_effects=True, vmem_limit_bytes=VMEM_LIMIT
        ),
        cost_estimate=pl.CostEstimate(
            flops=12 * slots * model * hidden, bytes_accessed=16 * model * hidden,
            transcendentals=0,
        ),
    )(
        query_input[0], key_input[0], value_input[0], routes[0].T, gate_values[0].T,
        up_weight[0], down_weight[0], cotangent[0],
    )
    return (
        layer[None], grad_q[None], grad_k[None], grad_v[None], grad_up[None], grad_down[None]
    )


def solution(mesh):
    tokens = P(("dp", "expert"), "seq", None)
    weights = P("expert", None, None)
    in_specs = (tokens,) * 5 + (weights, weights, tokens)
    out_specs = (tokens,) * 4 + (P("expert", ("dp", "seq"), None), P("expert", None, ("dp", "seq")))
    return jax.shard_map(shards, mesh=mesh, in_specs=in_specs, out_specs=out_specs, check_vma=False)
```

```python
import functools
import math

import jax
import jax.numpy as jnp
from jax import lax
from jax.experimental import pallas as pl
from jax.experimental.pallas import tpu as pltpu
from jax.sharding import PartitionSpec as P

DH = 128
TOP = 2
EPSILON = 1e-06
GELU_COEF = math.sqrt(2.0 / math.pi)
MESH = pl.DeviceIdType.MESH
F32 = jnp.float32
BF16 = jnp.bfloat16
VMEM_LIMIT = 60 * 1024 * 1024


def gelu_pair(inputs):
    square = inputs * inputs
    hyper = jnp.tanh(GELU_COEF * inputs * (1.0 + 0.044715 * square))
    half = 0.5 * (1.0 + hyper)
    result = inputs * half
    slope = half + 0.5 * inputs * (1.0 - hyper * hyper) * GELU_COEF * (
        1.0 + 3.0 * 0.044715 * square
    )
    return result, slope


def dot_nn(a, b):
    return jnp.dot(a, b, preferred_element_type=F32)


def dot_nt(a, b):
    return lax.dot_general(a, b, (((1,), (1,)), ((), ())), preferred_element_type=F32)


def dot_tn(a, b):
    return lax.dot_general(a, b, (((0,), (0,)), ((), ())), preferred_element_type=F32)


def greet(axes):
    barrier = pltpu.get_barrier_semaphore()
    total = 0
    for axis in axes:
        size = lax.axis_size(axis)
        me = lax.axis_index(axis)
        for step in range(1, size):
            peer = lax.rem(me + step, size)
            pl.semaphore_signal(barrier, inc=1, device_id={axis: peer}, device_id_type=MESH)
            total += 1
    pl.semaphore_wait(barrier, total)


def remote(src, dst, send, recv, axis, peer):
    return pltpu.make_async_remote_copy(
        src_ref=src,
        dst_ref=dst,
        send_sem=send,
        recv_sem=recv,
        device_id={axis: peer},
        device_id_type=MESH,
    )


def rows_of(index, count):
    return pl.ds(pl.multiple_of(index * count, count), count)


def split_cols(src, dst, send, recv, me, size, own_sem):
    rows = src.shape[0]
    width = src.shape[1] // size
    copies = []
    for step in range(1, size):
        peer = lax.rem(me + step, size)
        copy = remote(
            src.at[:, rows_of(peer, width)],
            dst.at[rows_of(me, rows), :],
            send.at[step],
            recv.at[step],
            "seq",
            peer,
        )
        copy.start()
        copies.append(copy)
    own = pltpu.make_async_copy(src.at[:, rows_of(me, width)], dst.at[rows_of(me, rows), :], own_sem)
    own.start()
    return copies, own


def join_block(src, dst, send, recv, me, size, step):
    rows = dst.shape[0]
    width = src.shape[1]
    peer = lax.rem(me + step, size)
    copy = remote(
        src.at[rows_of(peer, rows), :],
        dst.at[:, rows_of(me, width)],
        send.at[step],
        recv.at[step],
        "seq",
        peer,
    )
    copy.start()
    return copy


def join_rows(src, dst, send, recv, me, size):
    rows = dst.shape[0]
    width = src.shape[1]
    copies = [join_block(src, dst, send, recv, me, size, step) for step in range(1, size)]
    dst[:, rows_of(me, width)] = src[rows_of(me, rows), :]
    return copies


def swap_slots(src, dst, send, recv, me, size):
    cap = src.shape[0] // size
    copies = []
    for step in range(1, size):
        peer = lax.rem(me + step, size)
        copy = remote(
            src.at[rows_of(peer, cap), :],
            dst.at[rows_of(me, cap), :],
            send.at[step],
            recv.at[step],
            "expert",
            peer,
        )
        copy.start()
        copies.append(copy)
    dst[rows_of(me, cap), :] = src[rows_of(me, cap), :]
    return copies


def arrive(copies):
    for copy in copies:
        copy.wait_recv()


def softmax_rows(query, key):
    scores = dot_nt(query, key) * (1.0 / math.sqrt(DH))
    exponent = jnp.exp(scores - jnp.max(scores, axis=-1, keepdims=True))
    return exponent / jnp.sum(exponent, axis=-1, keepdims=True)


def as_column(row):
    size = row.shape[1]
    same = lax.broadcasted_iota(jnp.int32, (size, size), 0) == lax.broadcasted_iota(
        jnp.int32, (size, size), 1
    )
    return jnp.sum(jnp.where(same, row, 0.0), axis=1, keepdims=True)


def layer_kernel(
    experts, cap, chunk,
    q_hbm, k_hbm, v_hbm, routes_ref, gates_ref, up_hbm, down_hbm, cot_ref,
    layer_out, gq_out, gk_out, gv_out, gup_out, gdown_out,
    layer, gq, gk, gv, gup, gdown,
    qh, kh, vh, heads, att, probs, datt, dheads, gqh, gkh, gvh,
    place, sent_grad, grad_in, sent_rows, rows_in, out_rows, dnorm_rows, ret_out, ret_dnorm,
    up, down, dact, act, dpre, rows_t, grad_t,
    gw_own, gw_other, gw_recv, a1_recv, b1_recv, a2_sent, a2_recv, b2_sent, b2_recv,
    seq_send, seq_recv, exp_send, exp_recv, dp_send, dp_recv, red_send, red_recv, local_sem,
):
    n_seq = lax.axis_size("seq")
    n_exp = lax.axis_size("expert")
    me_seq = lax.axis_index("seq")
    me_exp = lax.axis_index("expert")
    me_dp = lax.axis_index("dp")
    rows = cot_ref.shape[0]
    slots = experts * cap
    model, hidden = up.shape
    width = heads.shape[1]
    n_heads = width // DH
    sent = []

    load_down = pltpu.make_async_copy(down_hbm, down, local_sem.at[0])
    load_up = pltpu.make_async_copy(up_hbm, up, local_sem.at[1])
    greet(("seq", "expert", "dp"))

    seq_copies = []
    own_copies = []
    for number, (src, dst) in enumerate(((q_hbm, qh), (k_hbm, kh), (v_hbm, vh))):
        copies, own = split_cols(
            src, dst, seq_send.at[number], seq_recv.at[number], me_seq, n_seq,
            local_sem.at[2 + number],
        )
        seq_copies += copies
        own_copies.append(own)
    load_down.start()
    load_up.start()

    expert_ids = lax.broadcasted_iota(jnp.int32, (experts, rows), 0)
    hits = [
        jnp.where(routes_ref[j : j + 1, :] == expert_ids, 1.0, 0.0).astype(F32)
        for j in range(TOP)
    ]
    earlier = lax.broadcasted_iota(jnp.int32, (rows, rows), 0) < lax.broadcasted_iota(
        jnp.int32, (rows, rows), 1
    )
    rank = dot_nn(
        (hits[0] + hits[1]).astype(BF16), jnp.where(earlier, 1.0, 0.0).astype(BF16)
    )
    base = rank + (expert_ids * cap).astype(F32)
    slot_ids = lax.broadcasted_iota(jnp.int32, (slots, rows), 0).astype(F32)
    cot = cot_ref[...].astype(F32)
    gates = [as_column(gates_ref[j : j + 1, :]) for j in range(TOP)]
    packed = None
    for j in range(TOP):
        slot = jnp.sum(hits[j] * base, axis=0, keepdims=True)
        place[j] = jnp.where(slot_ids == slot, 1.0, 0.0).astype(BF16)
        part = dot_nn(place[j], (gates[j] * cot).astype(BF16))
        packed = part if packed is None else packed + part
    sent_grad[...] = packed.astype(BF16)
    grad_copies = swap_slots(sent_grad, grad_in, exp_send.at[0], exp_recv.at[0], me_exp, n_exp)
    sent += seq_copies + grad_copies

    for own in own_copies:
        own.wait()
    arrive(seq_copies)
    back = []
    for step in [*range(1, n_seq), 0]:
        block = rows_of(lax.rem(me_seq + step, n_seq), rows)
        for head in range(n_heads):
            cols = slice(head * DH, (head + 1) * DH)
            prob = softmax_rows(qh[block, cols], kh[:, cols])
            probs[head, block, :] = prob
            heads[block, cols] = dot_nn(prob.astype(BF16), vh[:, cols]).astype(BF16)
        if step > 0:
            back.append(
                join_block(heads, att, seq_send.at[3], seq_recv.at[3], me_seq, n_seq, step)
            )
        else:
            att[:, rows_of(me_seq, width)] = heads[block, :]
    arrive(back)
    sent += back

    att_f = att[...].astype(F32)
    inverse = lax.rsqrt(jnp.mean(att_f * att_f, axis=-1, keepdims=True) + EPSILON)
    placer = place[0] + place[1]
    sent_rows[...] = dot_nn(placer, (att_f * inverse).astype(BF16)).astype(BF16)
    row_copies = swap_slots(sent_rows, rows_in, exp_send.at[1], exp_recv.at[1], me_exp, n_exp)
    sent += row_copies
    arrive(grad_copies)
    load_down.wait()
    load_up.wait()

    @pl.loop(0, hidden // chunk)
    def _(c):
        cols = rows_of(c, chunk)
        dact[:, cols] = dot_nt(grad_in[...], down[cols, :])

    grad_t[...] = grad_in[...].T
    arrive(row_copies)

    @pl.loop(0, hidden // chunk)
    def _(c):
        cols = rows_of(c, chunk)
        value, slope = gelu_pair(dot_nn(rows_in[...], up[:, cols]))
        act[:, cols] = value.astype(BF16)
        dpre[:, cols] = (dact[:, cols] * slope).astype(BF16)

    rows_t[...] = rows_in[...].T
    half = model // 2
    piece = half // n_seq
    pair = 2 * piece
    low = lax.rem(me_seq, 2)
    high = me_seq // 2
    peer_low = 2 * high + 1 - low
    peer_high = 2 * (1 - high) + low

    def grads_first(dst, core, bit):
        left = jnp.concatenate(
            [rows_t[rows_of(core * n_seq + 2 * n + bit, piece), :] for n in range(2)], axis=0
        )

        @pl.loop(0, hidden // chunk)
        def _(c):
            cols = rows_of(c, chunk)
            dst[:, cols] = dot_nn(left, dpre[:, cols]).astype(BF16)

    def grads_second(dst, core, bit):
        left = grad_t[rows_of(core * (n_seq // 2) + bit, pair), :]

        @pl.loop(0, hidden // chunk)
        def _(c):
            cols = rows_of(c, chunk)
            dst[:, cols] = dot_nn(left, act[:, cols]).astype(BF16)

    def core_send(number):
        copy = remote(
            gw_other.at[number], gw_recv.at[number], dp_send.at[number], dp_recv.at[number],
            "dp", 1 - me_dp,
        )
        copy.start()
        sent.append(copy)
        return copy

    def add_core(number):
        @pl.loop(0, hidden // chunk)
        def _(c):
            cols = rows_of(c, chunk)
            gw_own[number, :, cols] = (
                gw_own[number, :, cols].astype(F32) + gw_recv[number, :, cols].astype(F32)
            ).astype(BF16)

    def reduce_send(src, dst, number, peer):
        copy = remote(src, dst, red_send.at[number], red_recv.at[number], "seq", peer)
        copy.start()
        sent.append(copy)
        return copy

    grads_first(gw_other.at[0], 1 - me_dp, 1 - low)
    core_first = core_send(0)
    grads_second(gw_other.at[1], 1 - me_dp, 1 - high)
    core_second = core_send(1)
    grads_first(gw_own.at[0], me_dp, 1 - low)
    grads_second(gw_own.at[1], me_dp, 1 - high)

    @pl.loop(0, model // 256)
    def _(c):
        cols = rows_of(c, 256)
        dnorm_rows[:, cols] = dot_nt(dpre[...], up[cols, :]).astype(BF16)

    dnorm_copies = swap_slots(
        dnorm_rows, ret_dnorm, exp_send.at[2], exp_recv.at[2], me_exp, n_exp
    )
    sent += dnorm_copies

    core_first.wait_recv()
    add_core(0)
    a1 = []
    for number, which in enumerate((1 - high, high)):
        a1.append(
            reduce_send(gw_own.at[0, rows_of(which, piece), :], a1_recv.at[which], number, peer_low)
        )
    core_second.wait_recv()
    add_core(1)
    b1 = []
    for number, which in enumerate((1 - low, low), 2):
        b1.append(
            reduce_send(
                gw_own.at[1, rows_of(which, piece), :], b1_recv.at[which], number, peer_high
            )
        )

    grads_first(gw_other.at[2], 1 - me_dp, low)
    core_third = core_send(2)
    grads_second(gw_other.at[3], 1 - me_dp, high)
    core_fourth = core_send(3)
    grads_first(gw_own.at[2], me_dp, low)
    grads_second(gw_own.at[3], me_dp, high)

    @pl.loop(0, model // 256)
    def _(c):
        cols = rows_of(c, 256)
        out_rows[:, cols] = dot_nn(act[...], down[:, cols]).astype(BF16)

    core_third.wait_recv()
    add_core(2)
    core_fourth.wait_recv()
    add_core(3)

    arrive(dnorm_copies)
    out_copies = swap_slots(out_rows, ret_out, exp_send.at[3], exp_recv.at[3], me_exp, n_exp)
    sent += out_copies
    dunit = dot_tn(place[0] + place[1], ret_dnorm[...])
    att_f = att[...].astype(F32)
    inverse = lax.rsqrt(jnp.mean(att_f * att_f, axis=-1, keepdims=True) + EPSILON)
    unit = att_f * inverse
    datt[...] = (
        cot_ref[...].astype(F32)
        + inverse * (dunit - unit * jnp.mean(dunit * unit, axis=-1, keepdims=True))
    ).astype(BF16)
    datt_copies, own = split_cols(
        datt, dheads, seq_send.at[4], seq_recv.at[4], me_seq, n_seq, local_sem.at[5]
    )
    sent += datt_copies
    own.wait()
    arrive(datt_copies)

    scaling = 1.0 / math.sqrt(DH)
    for head in range(n_heads):
        cols = slice(head * DH, (head + 1) * DH)
        prob = probs[head]
        dhead = dheads[:, cols]
        gvh[:, cols] = dot_tn(prob.astype(BF16), dhead).astype(BF16)
        dprobs = dot_nt(dhead, vh[:, cols])
        delta = jnp.sum(prob * dprobs, axis=-1, keepdims=True)
        dscores = (prob * (dprobs - delta) * scaling).astype(BF16)
        gkh[:, cols] = dot_tn(dscores, qh[:, cols]).astype(BF16)
        gqh[:, cols] = dot_nn(dscores, kh[:, cols]).astype(BF16)
    last = []
    for number, (src, dst) in enumerate(((gvh, gv), (gkh, gk), (gqh, gq)), 5):
        last += join_rows(src, dst, seq_send.at[number], seq_recv.at[number], me_seq, n_seq)
    sent += last

    a1[0].wait_recv()
    a2_sent[...] = (
        gw_own[2, rows_of(1 - high, piece), :].astype(F32) + a1_recv[1 - high].astype(F32)
    ).astype(BF16)
    a2 = reduce_send(a2_sent, a2_recv, 4, peer_high)
    b1[0].wait_recv()
    b2_sent[...] = (
        gw_own[3, rows_of(1 - low, piece), :].astype(F32) + b1_recv[1 - low].astype(F32)
    ).astype(BF16)
    b2 = reduce_send(b2_sent, b2_recv, 5, peer_low)

    arrive(out_copies)
    mix = None
    for j in range(TOP):
        part = as_column(gates_ref[j : j + 1, :]) * dot_tn(place[j], ret_out[...])
        mix = part if mix is None else mix + part
    layer[...] = (att[...].astype(F32) + mix).astype(BF16)
    stores = []

    def store(src, dst):
        copy = pltpu.make_async_copy(src, dst, local_sem.at[6 + len(stores)])
        copy.start()
        stores.append(copy)

    store(layer, layer_out)
    a1[1].wait_recv()
    b1[1].wait_recv()
    for number, (src, dst) in enumerate(((gv, gv_out), (gk, gk_out), (gq, gq_out))):
        arrive(last[number * (n_seq - 1) : (number + 1) * (n_seq - 1)])
        store(src, dst)
    a2.wait_recv()
    gup[...] = (
        gw_own[2, rows_of(high, piece), :].astype(F32)
        + a1_recv[high].astype(F32)
        + a2_recv[...].astype(F32)
    )
    store(gup, gup_out)
    b2.wait_recv()
    gdown[...] = (
        gw_own[3, rows_of(low, piece), :].astype(F32)
        + b1_recv[low].astype(F32)
        + b2_recv[...].astype(F32)
    ).T
    store(gdown, gdown_out)
    for copy in sent:
        copy.wait_send()
    for copy in stores:
        copy.wait()


def copy_kernel(*refs):
    count = (len(refs) - 1) // 2
    sems = refs[-1]
    copies = [
        pltpu.make_async_copy(refs[n], refs[count + n], sems.at[n]) for n in range(count)
    ]
    for copy in copies:
        copy.start()
    for copy in copies:
        copy.wait()


def shards(
    query_input, key_input, value_input, routes, gate_values, up_weight, down_weight, cotangent
):
    rows, model = query_input.shape[1:]
    n_seq = lax.axis_size("seq")
    n_exp = lax.axis_size("expert")
    hidden = up_weight.shape[2]
    experts = up_weight.shape[0] * n_exp
    cap = rows * TOP * 3 // (2 * experts)
    cap = -(-cap // 16) * 16
    slots = experts * cap
    width = model // n_seq
    tokens = rows * n_seq
    half = model // 2
    piece = half // n_seq
    vmem = pl.BlockSpec(memory_space=pltpu.VMEM)
    hbm = pl.BlockSpec(memory_space=pl.ANY)
    dma = pltpu.SemaphoreType.DMA

    def shape(*dims, dtype=BF16):
        return jax.ShapeDtypeStruct(dims, dtype)

    def buf(*dims, dtype=BF16):
        return pltpu.VMEM(dims, dtype)

    head_block = buf(tokens, width)
    slot_block = buf(slots, model)
    row_block = buf(rows, model)
    out_shapes = [shape(rows, model)] * 4 + [
        shape(piece, hidden, dtype=F32),
        shape(hidden, piece, dtype=F32),
    ]
    results = pl.pallas_call(
        functools.partial(layer_kernel, experts, cap, 512),
        name="layer",
        out_shape=out_shapes,
        in_specs=[hbm] * 3 + [vmem] * 2 + [hbm] * 2 + [vmem],
        out_specs=[hbm] * 6,
        scratch_shapes=[
            row_block, row_block, row_block, row_block,
            buf(piece, hidden, dtype=F32),
            buf(hidden, piece, dtype=F32),
            head_block, head_block, head_block, head_block,
            buf(rows, model),
            buf(width // DH, tokens, tokens, dtype=F32),
            buf(rows, model),
            head_block, head_block, head_block, head_block,
            buf(TOP, slots, rows),
            slot_block, slot_block, slot_block, slot_block,
            slot_block, slot_block, slot_block, slot_block,
            buf(model, hidden),
            buf(hidden, model),
            buf(slots, hidden, dtype=F32),
            buf(slots, hidden),
            buf(slots, hidden),
            buf(model, slots),
            buf(model, slots),
            buf(4, 2 * piece, hidden),
            buf(4, 2 * piece, hidden),
            buf(4, 2 * piece, hidden),
            buf(2, piece, hidden),
            buf(2, piece, hidden),
            buf(piece, hidden), buf(piece, hidden), buf(piece, hidden), buf(piece, hidden),
            dma((8, n_seq)),
            dma((8, n_seq)),
            dma((4, n_exp)),
            dma((4, n_exp)),
            dma((4,)),
            dma((4,)),
            dma((6,)),
            dma((6,)),
            dma((12,)),
        ],
        compiler_params=pltpu.CompilerParams(
            collective_id=0, has_side_effects=True, vmem_limit_bytes=VMEM_LIMIT
        ),
        cost_estimate=pl.CostEstimate(
            flops=12 * slots * model * hidden, bytes_accessed=16 * model * hidden,
            transcendentals=0,
        ),
    )(
        query_input[0], key_input[0], value_input[0], routes[0].T, gate_values[0].T,
        up_weight[0], down_weight[0], cotangent[0],
    )
    results = pl.pallas_call(
        copy_kernel,
        name="outputs",
        out_shape=out_shapes,
        in_specs=[hbm] * 6,
        out_specs=[hbm] * 6,
        scratch_shapes=[dma((6,))],
        compiler_params=pltpu.CompilerParams(vmem_limit_bytes=VMEM_LIMIT),
    )(*results)
    return tuple(result[None] for result in results)


def solution(mesh):
    tokens = P(("dp", "expert"), "seq", None)
    weights = P("expert", None, None)
    in_specs = (tokens,) * 5 + (weights, weights, tokens)
    out_specs = (tokens,) * 4 + (P("expert", ("dp", "seq"), None), P("expert", None, ("dp", "seq")))
    return jax.shard_map(shards, mesh=mesh, in_specs=in_specs, out_specs=out_specs, check_vma=False)
```

```python
import functools
import math

import jax
import jax.numpy as jnp
from jax import lax
from jax.experimental import pallas as pl
from jax.experimental.pallas import tpu as pltpu
from jax.sharding import PartitionSpec as P

DH = 128
TOP = 2
EPSILON = 1e-06
GELU_COEF = math.sqrt(2.0 / math.pi)
MESH = pl.DeviceIdType.MESH
F32 = jnp.float32
BF16 = jnp.bfloat16
VMEM_LIMIT = 60 * 1024 * 1024


def gelu_pair(inputs):
    square = inputs * inputs
    hyper = jnp.tanh(GELU_COEF * inputs * (1.0 + 0.044715 * square))
    half = 0.5 * (1.0 + hyper)
    result = inputs * half
    slope = half + 0.5 * inputs * (1.0 - hyper * hyper) * GELU_COEF * (
        1.0 + 3.0 * 0.044715 * square
    )
    return result, slope


def dot_nn(a, b):
    return jnp.dot(a, b, preferred_element_type=F32)


def dot_nt(a, b):
    return lax.dot_general(a, b, (((1,), (1,)), ((), ())), preferred_element_type=F32)


def dot_tn(a, b):
    return lax.dot_general(a, b, (((0,), (0,)), ((), ())), preferred_element_type=F32)


def greet(axes):
    barrier = pltpu.get_barrier_semaphore()
    total = 0
    for axis in axes:
        size = lax.axis_size(axis)
        me = lax.axis_index(axis)
        for step in range(1, size):
            peer = lax.rem(me + step, size)
            pl.semaphore_signal(barrier, inc=1, device_id={axis: peer}, device_id_type=MESH)
            total += 1
    pl.semaphore_wait(barrier, total)


def remote(src, dst, send, recv, axis, peer):
    return pltpu.make_async_remote_copy(
        src_ref=src,
        dst_ref=dst,
        send_sem=send,
        recv_sem=recv,
        device_id={axis: peer},
        device_id_type=MESH,
    )


def rows_of(index, count):
    return pl.ds(pl.multiple_of(index * count, count), count)


def split_cols(src, dst, send, recv, me, size, own_sem):
    rows = src.shape[0]
    width = src.shape[1] // size
    copies = []
    for step in range(1, size):
        peer = lax.rem(me + step, size)
        copy = remote(
            src.at[:, rows_of(peer, width)],
            dst.at[rows_of(me, rows), :],
            send.at[step],
            recv.at[step],
            "seq",
            peer,
        )
        copy.start()
        copies.append(copy)
    own = pltpu.make_async_copy(src.at[:, rows_of(me, width)], dst.at[rows_of(me, rows), :], own_sem)
    own.start()
    return copies, own


def join_block(src, dst, send, recv, me, size, step):
    rows = dst.shape[0]
    width = src.shape[1]
    peer = lax.rem(me + step, size)
    copy = remote(
        src.at[rows_of(peer, rows), :],
        dst.at[:, rows_of(me, width)],
        send.at[step],
        recv.at[step],
        "seq",
        peer,
    )
    copy.start()
    return copy


def join_rows(src, dst, send, recv, me, size):
    rows = dst.shape[0]
    width = src.shape[1]
    copies = [join_block(src, dst, send, recv, me, size, step) for step in range(1, size)]
    dst[:, rows_of(me, width)] = src[rows_of(me, rows), :]
    return copies


def swap_slots(src, dst, send, recv, me, size):
    cap = src.shape[0] // size
    copies = []
    for step in range(1, size):
        peer = lax.rem(me + step, size)
        copy = remote(
            src.at[rows_of(peer, cap), :],
            dst.at[rows_of(me, cap), :],
            send.at[step],
            recv.at[step],
            "expert",
            peer,
        )
        copy.start()
        copies.append(copy)
    dst[rows_of(me, cap), :] = src[rows_of(me, cap), :]
    return copies


def arrive(copies):
    for copy in copies:
        copy.wait_recv()


def softmax_rows(query, key):
    scores = dot_nt(query, key) * (1.0 / math.sqrt(DH))
    exponent = jnp.exp(scores - jnp.max(scores, axis=-1, keepdims=True))
    return exponent / jnp.sum(exponent, axis=-1, keepdims=True)


def as_column(row):
    size = row.shape[1]
    same = lax.broadcasted_iota(jnp.int32, (size, size), 0) == lax.broadcasted_iota(
        jnp.int32, (size, size), 1
    )
    return jnp.sum(jnp.where(same, row, 0.0), axis=1, keepdims=True)


def layer_kernel(
    experts, cap, chunk,
    q_hbm, k_hbm, v_hbm, routes_ref, gates_ref, up_hbm, down_hbm, cot_ref,
    layer_out, gq_out, gk_out, gv_out, gup_out, gdown_out,
    layer, gq, gk, gv, gup, gdown,
    qh, kh, vh, heads, att, probs, datt, dheads, gqh, gkh, gvh,
    place, sent_grad, grad_in, sent_rows, rows_in, out_rows, dnorm_rows, ret_out, ret_dnorm,
    up, down, dact, act, dpre, rows_t, grad_t,
    gw_own, gw_other, gw_recv, a1_recv, b1_recv, a2_sent, a2_recv, b2_sent, b2_recv,
    seq_send, seq_recv, exp_send, exp_recv, dp_send, dp_recv, red_send, red_recv, local_sem,
):
    n_seq = lax.axis_size("seq")
    n_exp = lax.axis_size("expert")
    me_seq = lax.axis_index("seq")
    me_exp = lax.axis_index("expert")
    me_dp = lax.axis_index("dp")
    rows = cot_ref.shape[0]
    slots = experts * cap
    model, hidden = up.shape
    width = heads.shape[1]
    n_heads = width // DH
    sent = []

    load_down = pltpu.make_async_copy(down_hbm, down, local_sem.at[0])
    load_up = pltpu.make_async_copy(up_hbm, up, local_sem.at[1])
    greet(("seq", "expert", "dp"))

    seq_copies = []
    own_copies = []
    for number, (src, dst) in enumerate(((q_hbm, qh), (k_hbm, kh), (v_hbm, vh))):
        copies, own = split_cols(
            src, dst, seq_send.at[number], seq_recv.at[number], me_seq, n_seq,
            local_sem.at[2 + number],
        )
        seq_copies += copies
        own_copies.append(own)
    load_down.start()
    load_up.start()

    expert_ids = lax.broadcasted_iota(jnp.int32, (experts, rows), 0)
    hits = [
        jnp.where(routes_ref[j : j + 1, :] == expert_ids, 1.0, 0.0).astype(F32)
        for j in range(TOP)
    ]
    earlier = lax.broadcasted_iota(jnp.int32, (rows, rows), 0) < lax.broadcasted_iota(
        jnp.int32, (rows, rows), 1
    )
    rank = dot_nn(
        (hits[0] + hits[1]).astype(BF16), jnp.where(earlier, 1.0, 0.0).astype(BF16)
    )
    base = rank + (expert_ids * cap).astype(F32)
    slot_ids = lax.broadcasted_iota(jnp.int32, (slots, rows), 0).astype(F32)
    cot = cot_ref[...].astype(F32)
    gates = [as_column(gates_ref[j : j + 1, :]) for j in range(TOP)]
    packed = None
    for j in range(TOP):
        slot = jnp.sum(hits[j] * base, axis=0, keepdims=True)
        place[j] = jnp.where(slot_ids == slot, 1.0, 0.0).astype(BF16)
        part = dot_nn(place[j], (gates[j] * cot).astype(BF16))
        packed = part if packed is None else packed + part
    sent_grad[...] = packed.astype(BF16)
    grad_copies = swap_slots(sent_grad, grad_in, exp_send.at[0], exp_recv.at[0], me_exp, n_exp)
    sent += seq_copies + grad_copies

    for own in own_copies:
        own.wait()
    arrive(seq_copies)
    back = []
    for step in [*range(1, n_seq), 0]:
        block = rows_of(lax.rem(me_seq + step, n_seq), rows)
        for head in range(n_heads):
            cols = slice(head * DH, (head + 1) * DH)
            prob = softmax_rows(qh[block, cols], kh[:, cols])
            probs[head, block, :] = prob
            heads[block, cols] = dot_nn(prob.astype(BF16), vh[:, cols]).astype(BF16)
        if step > 0:
            back.append(
                join_block(heads, att, seq_send.at[3], seq_recv.at[3], me_seq, n_seq, step)
            )
        else:
            att[:, rows_of(me_seq, width)] = heads[block, :]
    arrive(back)
    sent += back

    att_f = att[...].astype(F32)
    inverse = lax.rsqrt(jnp.mean(att_f * att_f, axis=-1, keepdims=True) + EPSILON)
    placer = place[0] + place[1]
    sent_rows[...] = dot_nn(placer, (att_f * inverse).astype(BF16)).astype(BF16)
    row_copies = swap_slots(sent_rows, rows_in, exp_send.at[1], exp_recv.at[1], me_exp, n_exp)
    sent += row_copies
    arrive(grad_copies)
    load_down.wait()
    load_up.wait()

    @pl.loop(0, hidden // chunk)
    def _(c):
        cols = rows_of(c, chunk)
        dact[:, cols] = dot_nt(grad_in[...], down[cols, :])

    grad_t[...] = grad_in[...].T
    arrive(row_copies)

    @pl.loop(0, hidden // chunk)
    def _(c):
        cols = rows_of(c, chunk)
        value, slope = gelu_pair(dot_nn(rows_in[...], up[:, cols]))
        act[:, cols] = value.astype(BF16)
        dpre[:, cols] = (dact[:, cols] * slope).astype(BF16)

    rows_t[...] = rows_in[...].T
    half = model // 2
    piece = half // n_seq
    pair = 2 * piece
    low = lax.rem(me_seq, 2)
    high = me_seq // 2
    peer_low = 2 * high + 1 - low
    peer_high = 2 * (1 - high) + low

    def grads_first(dst, core, bit):
        left = jnp.concatenate(
            [rows_t[rows_of(core * n_seq + 2 * n + bit, piece), :] for n in range(2)], axis=0
        )

        @pl.loop(0, hidden // chunk)
        def _(c):
            cols = rows_of(c, chunk)
            dst[:, cols] = dot_nn(left, dpre[:, cols]).astype(BF16)

    def grads_second(dst, core, bit):
        left = grad_t[rows_of(core * (n_seq // 2) + bit, pair), :]

        @pl.loop(0, hidden // chunk)
        def _(c):
            cols = rows_of(c, chunk)
            dst[:, cols] = dot_nn(left, act[:, cols]).astype(BF16)

    def core_send(number):
        copy = remote(
            gw_other.at[number], gw_recv.at[number], dp_send.at[number], dp_recv.at[number],
            "dp", 1 - me_dp,
        )
        copy.start()
        sent.append(copy)
        return copy

    def add_core(number):
        @pl.loop(0, hidden // chunk)
        def _(c):
            cols = rows_of(c, chunk)
            gw_own[number, :, cols] = (
                gw_own[number, :, cols].astype(F32) + gw_recv[number, :, cols].astype(F32)
            ).astype(BF16)

    def reduce_send(src, dst, number, peer):
        copy = remote(src, dst, red_send.at[number], red_recv.at[number], "seq", peer)
        copy.start()
        sent.append(copy)
        return copy

    grads_first(gw_other.at[0], 1 - me_dp, 1 - low)
    core_first = core_send(0)
    grads_second(gw_other.at[1], 1 - me_dp, 1 - high)
    core_second = core_send(1)
    grads_first(gw_own.at[0], me_dp, 1 - low)
    grads_second(gw_own.at[1], me_dp, 1 - high)

    @pl.loop(0, model // 256)
    def _(c):
        cols = rows_of(c, 256)
        dnorm_rows[:, cols] = dot_nt(dpre[...], up[cols, :]).astype(BF16)

    dnorm_copies = swap_slots(
        dnorm_rows, ret_dnorm, exp_send.at[2], exp_recv.at[2], me_exp, n_exp
    )
    sent += dnorm_copies

    core_first.wait_recv()
    add_core(0)
    a1 = []
    for number, which in enumerate((1 - high, high)):
        a1.append(
            reduce_send(gw_own.at[0, rows_of(which, piece), :], a1_recv.at[which], number, peer_low)
        )
    core_second.wait_recv()
    add_core(1)
    b1 = []
    for number, which in enumerate((1 - low, low), 2):
        b1.append(
            reduce_send(
                gw_own.at[1, rows_of(which, piece), :], b1_recv.at[which], number, peer_high
            )
        )

    grads_first(gw_other.at[2], 1 - me_dp, low)
    core_third = core_send(2)
    grads_second(gw_other.at[3], 1 - me_dp, high)
    core_fourth = core_send(3)
    grads_first(gw_own.at[2], me_dp, low)
    grads_second(gw_own.at[3], me_dp, high)

    @pl.loop(0, model // 256)
    def _(c):
        cols = rows_of(c, 256)
        out_rows[:, cols] = dot_nn(act[...], down[:, cols]).astype(BF16)

    core_third.wait_recv()
    add_core(2)
    core_fourth.wait_recv()
    add_core(3)

    arrive(dnorm_copies)
    out_copies = swap_slots(out_rows, ret_out, exp_send.at[3], exp_recv.at[3], me_exp, n_exp)
    sent += out_copies
    dunit = dot_tn(place[0] + place[1], ret_dnorm[...])
    att_f = att[...].astype(F32)
    inverse = lax.rsqrt(jnp.mean(att_f * att_f, axis=-1, keepdims=True) + EPSILON)
    unit = att_f * inverse
    datt[...] = (
        cot_ref[...].astype(F32)
        + inverse * (dunit - unit * jnp.mean(dunit * unit, axis=-1, keepdims=True))
    ).astype(BF16)
    datt_copies, own = split_cols(
        datt, dheads, seq_send.at[4], seq_recv.at[4], me_seq, n_seq, local_sem.at[5]
    )
    sent += datt_copies
    own.wait()
    arrive(datt_copies)

    scaling = 1.0 / math.sqrt(DH)
    for head in range(n_heads):
        cols = slice(head * DH, (head + 1) * DH)
        prob = probs[head]
        dhead = dheads[:, cols]
        gvh[:, cols] = dot_tn(prob.astype(BF16), dhead).astype(BF16)
        dprobs = dot_nt(dhead, vh[:, cols])
        delta = jnp.sum(prob * dprobs, axis=-1, keepdims=True)
        dscores = (prob * (dprobs - delta) * scaling).astype(BF16)
        gkh[:, cols] = dot_tn(dscores, qh[:, cols]).astype(BF16)
        gqh[:, cols] = dot_nn(dscores, kh[:, cols]).astype(BF16)
    last = []
    for number, (src, dst) in enumerate(((gvh, gv), (gkh, gk), (gqh, gq)), 5):
        last += join_rows(src, dst, seq_send.at[number], seq_recv.at[number], me_seq, n_seq)
    sent += last

    a1[0].wait_recv()
    a2_sent[...] = (
        gw_own[2, rows_of(1 - high, piece), :].astype(F32) + a1_recv[1 - high].astype(F32)
    ).astype(BF16)
    a2 = reduce_send(a2_sent, a2_recv, 4, peer_high)
    b1[0].wait_recv()
    b2_sent[...] = (
        gw_own[3, rows_of(1 - low, piece), :].astype(F32) + b1_recv[1 - low].astype(F32)
    ).astype(BF16)
    b2 = reduce_send(b2_sent, b2_recv, 5, peer_low)

    arrive(out_copies)
    mix = None
    for j in range(TOP):
        part = as_column(gates_ref[j : j + 1, :]) * dot_tn(place[j], ret_out[...])
        mix = part if mix is None else mix + part
    layer[...] = (att[...].astype(F32) + mix).astype(BF16)
    stores = []

    def store(src, dst):
        copy = pltpu.make_async_copy(src, dst, local_sem.at[6 + len(stores)])
        copy.start()
        stores.append(copy)

    store(layer, layer_out)
    a1[1].wait_recv()
    b1[1].wait_recv()
    for number, (src, dst) in enumerate(((gv, gv_out), (gk, gk_out), (gq, gq_out))):
        arrive(last[number * (n_seq - 1) : (number + 1) * (n_seq - 1)])
        store(src, dst)
    a2.wait_recv()
    gup[...] = (
        gw_own[2, rows_of(high, piece), :].astype(F32)
        + a1_recv[high].astype(F32)
        + a2_recv[...].astype(F32)
    )
    store(gup, gup_out)
    b2.wait_recv()
    gdown[...] = (
        gw_own[3, rows_of(low, piece), :].astype(F32)
        + b1_recv[low].astype(F32)
        + b2_recv[...].astype(F32)
    ).T
    store(gdown, gdown_out)
    for copy in sent:
        copy.wait_send()
    for copy in stores:
        copy.wait()


def copy_kernel(*refs):
    count = (len(refs) - 1) // 3
    sources, targets, held, sems = refs[:count], refs[count : 2 * count], refs[2 * count : -1], refs[-1]
    loads = [
        pltpu.make_async_copy(sources[n], held[n], sems.at[n]) for n in range(count)
    ]
    saves = [
        pltpu.make_async_copy(held[n], targets[n], sems.at[count + n]) for n in range(count)
    ]
    for load in loads:
        load.start()
    for load, save in zip(loads, saves):
        load.wait()
        save.start()
    for save in saves:
        save.wait()


def shards(
    query_input, key_input, value_input, routes, gate_values, up_weight, down_weight, cotangent
):
    rows, model = query_input.shape[1:]
    n_seq = lax.axis_size("seq")
    n_exp = lax.axis_size("expert")
    hidden = up_weight.shape[2]
    experts = up_weight.shape[0] * n_exp
    cap = rows * TOP * 3 // (2 * experts)
    cap = -(-cap // 16) * 16
    slots = experts * cap
    width = model // n_seq
    tokens = rows * n_seq
    half = model // 2
    piece = half // n_seq
    vmem = pl.BlockSpec(memory_space=pltpu.VMEM)
    hbm = pl.BlockSpec(memory_space=pl.ANY)
    dma = pltpu.SemaphoreType.DMA

    def shape(*dims, dtype=BF16):
        return jax.ShapeDtypeStruct(dims, dtype)

    def buf(*dims, dtype=BF16):
        return pltpu.VMEM(dims, dtype)

    head_block = buf(tokens, width)
    slot_block = buf(slots, model)
    row_block = buf(rows, model)
    out_shapes = [shape(rows, model)] * 4 + [
        shape(piece, hidden, dtype=F32),
        shape(hidden, piece, dtype=F32),
    ]
    results = pl.pallas_call(
        functools.partial(layer_kernel, experts, cap, 512),
        name="layer",
        out_shape=out_shapes,
        in_specs=[hbm] * 3 + [vmem] * 2 + [hbm] * 2 + [vmem],
        out_specs=[hbm] * 6,
        scratch_shapes=[
            row_block, row_block, row_block, row_block,
            buf(piece, hidden, dtype=F32),
            buf(hidden, piece, dtype=F32),
            head_block, head_block, head_block, head_block,
            buf(rows, model),
            buf(width // DH, tokens, tokens, dtype=F32),
            buf(rows, model),
            head_block, head_block, head_block, head_block,
            buf(TOP, slots, rows),
            slot_block, slot_block, slot_block, slot_block,
            slot_block, slot_block, slot_block, slot_block,
            buf(model, hidden),
            buf(hidden, model),
            buf(slots, hidden, dtype=F32),
            buf(slots, hidden),
            buf(slots, hidden),
            buf(model, slots),
            buf(model, slots),
            buf(4, 2 * piece, hidden),
            buf(4, 2 * piece, hidden),
            buf(4, 2 * piece, hidden),
            buf(2, piece, hidden),
            buf(2, piece, hidden),
            buf(piece, hidden), buf(piece, hidden), buf(piece, hidden), buf(piece, hidden),
            dma((8, n_seq)),
            dma((8, n_seq)),
            dma((4, n_exp)),
            dma((4, n_exp)),
            dma((4,)),
            dma((4,)),
            dma((6,)),
            dma((6,)),
            dma((12,)),
        ],
        compiler_params=pltpu.CompilerParams(
            collective_id=0, has_side_effects=True, vmem_limit_bytes=VMEM_LIMIT
        ),
        cost_estimate=pl.CostEstimate(
            flops=12 * slots * model * hidden, bytes_accessed=16 * model * hidden,
            transcendentals=0,
        ),
    )(
        query_input[0], key_input[0], value_input[0], routes[0].T, gate_values[0].T,
        up_weight[0], down_weight[0], cotangent[0],
    )
    results = pl.pallas_call(
        copy_kernel,
        name="outputs",
        out_shape=out_shapes,
        in_specs=[hbm] * 6,
        out_specs=[hbm] * 6,
        scratch_shapes=[pltpu.VMEM(out.shape, out.dtype) for out in out_shapes] + [dma((12,))],
        compiler_params=pltpu.CompilerParams(vmem_limit_bytes=VMEM_LIMIT),
    )(*results)
    return tuple(result[None] for result in results)


def solution(mesh):
    tokens = P(("dp", "expert"), "seq", None)
    weights = P("expert", None, None)
    in_specs = (tokens,) * 5 + (weights, weights, tokens)
    out_specs = (tokens,) * 4 + (P("expert", ("dp", "seq"), None), P("expert", None, ("dp", "seq")))
    return jax.shard_map(shards, mesh=mesh, in_specs=in_specs, out_specs=out_specs, check_vma=False)
```

```python
import functools
import math

import jax
import jax.numpy as jnp
from jax import lax
from jax.experimental import pallas as pl
from jax.experimental.pallas import tpu as pltpu
from jax.sharding import PartitionSpec as P

DH = 128
TOP = 2
EPSILON = 1e-06
GELU_COEF = math.sqrt(2.0 / math.pi)
MESH = pl.DeviceIdType.MESH
F32 = jnp.float32
BF16 = jnp.bfloat16
VMEM_LIMIT = 60 * 1024 * 1024


def gelu_pair(inputs):
    square = inputs * inputs
    hyper = jnp.tanh(GELU_COEF * inputs * (1.0 + 0.044715 * square))
    half = 0.5 * (1.0 + hyper)
    result = inputs * half
    slope = half + 0.5 * inputs * (1.0 - hyper * hyper) * GELU_COEF * (
        1.0 + 3.0 * 0.044715 * square
    )
    return result, slope


def dot_nn(a, b):
    return jnp.dot(a, b, preferred_element_type=F32)


def dot_nt(a, b):
    return lax.dot_general(a, b, (((1,), (1,)), ((), ())), preferred_element_type=F32)


def dot_tn(a, b):
    return lax.dot_general(a, b, (((0,), (0,)), ((), ())), preferred_element_type=F32)


def greet(axes):
    barrier = pltpu.get_barrier_semaphore()
    total = 0
    for axis in axes:
        size = lax.axis_size(axis)
        me = lax.axis_index(axis)
        for step in range(1, size):
            peer = lax.rem(me + step, size)
            pl.semaphore_signal(barrier, inc=1, device_id={axis: peer}, device_id_type=MESH)
            total += 1
    pl.semaphore_wait(barrier, total)


def remote(src, dst, send, recv, axis, peer):
    return pltpu.make_async_remote_copy(
        src_ref=src,
        dst_ref=dst,
        send_sem=send,
        recv_sem=recv,
        device_id={axis: peer},
        device_id_type=MESH,
    )


def rows_of(index, count):
    return pl.ds(pl.multiple_of(index * count, count), count)


def split_cols(src, dst, send, recv, me, size, own_sem):
    rows = src.shape[0]
    width = src.shape[1] // size
    copies = []
    for step in range(1, size):
        peer = lax.rem(me + step, size)
        copy = remote(
            src.at[:, rows_of(peer, width)],
            dst.at[rows_of(me, rows), :],
            send.at[step],
            recv.at[step],
            "seq",
            peer,
        )
        copy.start()
        copies.append(copy)
    own = pltpu.make_async_copy(src.at[:, rows_of(me, width)], dst.at[rows_of(me, rows), :], own_sem)
    own.start()
    return copies, own


def join_block(src, dst, send, recv, me, size, step):
    rows = dst.shape[0]
    width = src.shape[1]
    peer = lax.rem(me + step, size)
    copy = remote(
        src.at[rows_of(peer, rows), :],
        dst.at[:, rows_of(me, width)],
        send.at[step],
        recv.at[step],
        "seq",
        peer,
    )
    copy.start()
    return copy


def swap_slots(src, dst, send, recv, me, size):
    cap = src.shape[0] // size
    copies = []
    for step in range(1, size):
        peer = lax.rem(me + step, size)
        copy = remote(
            src.at[rows_of(peer, cap), :],
            dst.at[rows_of(me, cap), :],
            send.at[step],
            recv.at[step],
            "expert",
            peer,
        )
        copy.start()
        copies.append(copy)
    dst[rows_of(me, cap), :] = src[rows_of(me, cap), :]
    return copies


def arrive(copies):
    for copy in copies:
        copy.wait_recv()


def softmax_rows(query, key):
    scores = dot_nt(query, key) * (1.0 / math.sqrt(DH))
    exponent = jnp.exp(scores - jnp.max(scores, axis=-1, keepdims=True))
    return exponent / jnp.sum(exponent, axis=-1, keepdims=True)


def as_column(row):
    size = row.shape[1]
    same = lax.broadcasted_iota(jnp.int32, (size, size), 0) == lax.broadcasted_iota(
        jnp.int32, (size, size), 1
    )
    return jnp.sum(jnp.where(same, row, 0.0), axis=1, keepdims=True)


def layer_kernel(
    experts, cap, chunk,
    q_hbm, k_hbm, v_hbm, routes_ref, gates_ref, up_hbm, down_hbm, cot_ref,
    layer_out, gq_out, gk_out, gv_out, gup_out, gdown_out,
    layer, gq, gk, gv, gup, gdown,
    qh, kh, vh, heads, att, probs, probs_t, datt, dheads, gqh, gkh, gvh,
    place, sent_grad, grad_in, sent_rows, rows_in, out_rows, dnorm_rows, ret_out, ret_dnorm,
    up, down, dact, act, dpre, rows_t, grad_t,
    gw_own, gw_other, gw_recv, a1_recv, b1_recv, a2_sent, a2_recv, b2_sent, b2_recv,
    seq_send, seq_recv, exp_send, exp_recv, dp_send, dp_recv, red_send, red_recv, local_sem,
):
    n_seq = lax.axis_size("seq")
    n_exp = lax.axis_size("expert")
    me_seq = lax.axis_index("seq")
    me_exp = lax.axis_index("expert")
    me_dp = lax.axis_index("dp")
    rows = cot_ref.shape[0]
    slots = experts * cap
    model, hidden = up.shape
    width = heads.shape[1]
    n_heads = width // DH
    sent = []

    load_down = pltpu.make_async_copy(down_hbm, down, local_sem.at[0])
    load_up = pltpu.make_async_copy(up_hbm, up, local_sem.at[1])
    greet(("seq", "expert", "dp"))

    seq_copies = []
    own_copies = []
    for number, (src, dst) in enumerate(((q_hbm, qh), (k_hbm, kh), (v_hbm, vh))):
        copies, own = split_cols(
            src, dst, seq_send.at[number], seq_recv.at[number], me_seq, n_seq,
            local_sem.at[2 + number],
        )
        seq_copies += copies
        own_copies.append(own)
    load_down.start()
    load_up.start()

    expert_ids = lax.broadcasted_iota(jnp.int32, (experts, rows), 0)
    hits = [
        jnp.where(routes_ref[j : j + 1, :] == expert_ids, 1.0, 0.0).astype(F32)
        for j in range(TOP)
    ]
    earlier = lax.broadcasted_iota(jnp.int32, (rows, rows), 0) < lax.broadcasted_iota(
        jnp.int32, (rows, rows), 1
    )
    rank = dot_nn(
        (hits[0] + hits[1]).astype(BF16), jnp.where(earlier, 1.0, 0.0).astype(BF16)
    )
    base = rank + (expert_ids * cap).astype(F32)
    slot_ids = lax.broadcasted_iota(jnp.int32, (slots, rows), 0).astype(F32)
    cot = cot_ref[...].astype(F32)
    gates = [as_column(gates_ref[j : j + 1, :]) for j in range(TOP)]
    packed = None
    for j in range(TOP):
        slot = jnp.sum(hits[j] * base, axis=0, keepdims=True)
        place[j] = jnp.where(slot_ids == slot, 1.0, 0.0).astype(BF16)
        part = dot_nn(place[j], (gates[j] * cot).astype(BF16))
        packed = part if packed is None else packed + part
    sent_grad[...] = packed.astype(BF16)
    grad_copies = swap_slots(sent_grad, grad_in, exp_send.at[0], exp_recv.at[0], me_exp, n_exp)
    sent += seq_copies + grad_copies

    for own in own_copies:
        own.wait()
    arrive(seq_copies)
    back = []
    for step in [*range(1, n_seq), 0]:
        block = rows_of(lax.rem(me_seq + step, n_seq), rows)
        for head in range(n_heads):
            cols = slice(head * DH, (head + 1) * DH)
            prob = softmax_rows(qh[block, cols], kh[:, cols])
            probs[head, block, :] = prob
            heads[block, cols] = dot_nn(prob.astype(BF16), vh[:, cols]).astype(BF16)
        if step > 0:
            back.append(
                join_block(heads, att, seq_send.at[3], seq_recv.at[3], me_seq, n_seq, step)
            )
        else:
            att[:, rows_of(me_seq, width)] = heads[block, :]
    arrive(back)
    sent += back

    att_f = att[...].astype(F32)
    inverse = lax.rsqrt(jnp.mean(att_f * att_f, axis=-1, keepdims=True) + EPSILON)
    placer = place[0] + place[1]
    sent_rows[...] = dot_nn(placer, (att_f * inverse).astype(BF16)).astype(BF16)
    row_copies = swap_slots(sent_rows, rows_in, exp_send.at[1], exp_recv.at[1], me_exp, n_exp)
    sent += row_copies
    for head in range(n_heads):
        probs_t[head] = probs[head].astype(BF16).T
    arrive(grad_copies)
    load_down.wait()
    load_up.wait()

    @pl.loop(0, hidden // chunk)
    def _(c):
        cols = rows_of(c, chunk)
        dact[:, cols] = dot_nt(grad_in[...], down[cols, :])

    grad_t[...] = grad_in[...].T
    arrive(row_copies)

    @pl.loop(0, hidden // chunk)
    def _(c):
        cols = rows_of(c, chunk)
        value, slope = gelu_pair(dot_nn(rows_in[...], up[:, cols]))
        act[:, cols] = value.astype(BF16)
        dpre[:, cols] = (dact[:, cols] * slope).astype(BF16)

    rows_t[...] = rows_in[...].T
    half = model // 2
    piece = half // n_seq
    pair = 2 * piece
    low = lax.rem(me_seq, 2)
    high = me_seq // 2
    peer_low = 2 * high + 1 - low
    peer_high = 2 * (1 - high) + low

    def grads_first(dst, core, bit):
        left = jnp.concatenate(
            [rows_t[rows_of(core * n_seq + 2 * n + bit, piece), :] for n in range(2)], axis=0
        )

        @pl.loop(0, hidden // chunk)
        def _(c):
            cols = rows_of(c, chunk)
            dst[:, cols] = dot_nn(left, dpre[:, cols]).astype(BF16)

    def grads_second(dst, core, bit):
        left = grad_t[rows_of(core * (n_seq // 2) + bit, pair), :]

        @pl.loop(0, hidden // chunk)
        def _(c):
            cols = rows_of(c, chunk)
            dst[:, cols] = dot_nn(left, act[:, cols]).astype(BF16)

    def core_send(number):
        copy = remote(
            gw_other.at[number], gw_recv.at[number], dp_send.at[number], dp_recv.at[number],
            "dp", 1 - me_dp,
        )
        copy.start()
        sent.append(copy)
        return copy

    def add_core(number):
        @pl.loop(0, hidden // chunk)
        def _(c):
            cols = rows_of(c, chunk)
            gw_own[number, :, cols] = (
                gw_own[number, :, cols].astype(F32) + gw_recv[number, :, cols].astype(F32)
            ).astype(BF16)

    def reduce_send(src, dst, number, peer):
        copy = remote(src, dst, red_send.at[number], red_recv.at[number], "seq", peer)
        copy.start()
        sent.append(copy)
        return copy

    grads_first(gw_other.at[0], 1 - me_dp, 1 - low)
    core_first = core_send(0)
    grads_second(gw_other.at[1], 1 - me_dp, 1 - high)
    core_second = core_send(1)
    grads_first(gw_own.at[0], me_dp, 1 - low)
    grads_second(gw_own.at[1], me_dp, 1 - high)

    @pl.loop(0, model // 256)
    def _(c):
        cols = rows_of(c, 256)
        dnorm_rows[:, cols] = dot_nt(dpre[...], up[cols, :]).astype(BF16)

    dnorm_copies = swap_slots(
        dnorm_rows, ret_dnorm, exp_send.at[2], exp_recv.at[2], me_exp, n_exp
    )
    sent += dnorm_copies

    core_first.wait_recv()
    add_core(0)
    a1 = []
    for number, which in enumerate((1 - high, high)):
        a1.append(
            reduce_send(gw_own.at[0, rows_of(which, piece), :], a1_recv.at[which], number, peer_low)
        )
    core_second.wait_recv()
    add_core(1)
    b1 = []
    for number, which in enumerate((1 - low, low), 2):
        b1.append(
            reduce_send(
                gw_own.at[1, rows_of(which, piece), :], b1_recv.at[which], number, peer_high
            )
        )

    grads_first(gw_other.at[2], 1 - me_dp, low)
    core_third = core_send(2)
    grads_second(gw_other.at[3], 1 - me_dp, high)
    core_fourth = core_send(3)
    grads_first(gw_own.at[2], me_dp, low)
    grads_second(gw_own.at[3], me_dp, high)

    @pl.loop(0, model // 256)
    def _(c):
        cols = rows_of(c, 256)
        out_rows[:, cols] = dot_nn(act[...], down[:, cols]).astype(BF16)

    core_third.wait_recv()
    add_core(2)
    core_fourth.wait_recv()
    add_core(3)

    def join_head(src, dst, head, number):
        cols = slice(head * DH, (head + 1) * DH)
        there = pl.ds(pl.multiple_of(me_seq * width + head * DH, DH), DH)
        copies = []
        for step in range(1, n_seq):
            peer = lax.rem(me_seq + step, n_seq)
            copy = remote(
                src.at[rows_of(peer, rows), cols],
                dst.at[:, there],
                seq_send.at[number, step],
                seq_recv.at[number, step],
                "seq",
                peer,
            )
            copy.start()
            copies.append(copy)
        dst[:, there] = src[rows_of(me_seq, rows), cols]
        return copies

    arrive(dnorm_copies)
    out_copies = swap_slots(out_rows, ret_out, exp_send.at[3], exp_recv.at[3], me_exp, n_exp)
    sent += out_copies
    dunit = dot_tn(place[0] + place[1], ret_dnorm[...])
    att_f = att[...].astype(F32)
    inverse = lax.rsqrt(jnp.mean(att_f * att_f, axis=-1, keepdims=True) + EPSILON)
    unit = att_f * inverse
    datt[...] = (
        cot_ref[...].astype(F32)
        + inverse * (dunit - unit * jnp.mean(dunit * unit, axis=-1, keepdims=True))
    ).astype(BF16)
    datt_copies, own = split_cols(
        datt, dheads, seq_send.at[4], seq_recv.at[4], me_seq, n_seq, local_sem.at[5]
    )
    sent += datt_copies
    own.wait()
    arrive(datt_copies)

    scaling = 1.0 / math.sqrt(DH)
    last = []
    for head in range(n_heads):
        cols = slice(head * DH, (head + 1) * DH)
        prob = probs[head]
        dhead = dheads[:, cols]
        dprobs = dot_nt(dhead, vh[:, cols])
        gvh[:, cols] = dot_nn(probs_t[head], dhead).astype(BF16)
        last.append(join_head(gvh, gv, head, 5 + 3 * head))
        delta = jnp.sum(prob * dprobs, axis=-1, keepdims=True)
        dscores = (prob * (dprobs - delta) * scaling).astype(BF16)
        gqh[:, cols] = dot_nn(dscores, kh[:, cols]).astype(BF16)
        last.append(join_head(gqh, gq, head, 6 + 3 * head))
        gkh[:, cols] = dot_tn(dscores, qh[:, cols]).astype(BF16)
        last.append(join_head(gkh, gk, head, 7 + 3 * head))
        if head == 0:
            a1[0].wait_recv()
            a2_sent[...] = (
                gw_own[2, rows_of(1 - high, piece), :].astype(F32)
                + a1_recv[1 - high].astype(F32)
            ).astype(BF16)
            a2 = reduce_send(a2_sent, a2_recv, 4, peer_high)
            b1[0].wait_recv()
            b2_sent[...] = (
                gw_own[3, rows_of(1 - low, piece), :].astype(F32)
                + b1_recv[1 - low].astype(F32)
            ).astype(BF16)
            b2 = reduce_send(b2_sent, b2_recv, 5, peer_low)
    for copies in last:
        sent += copies

    arrive(out_copies)
    mix = None
    for j in range(TOP):
        part = as_column(gates_ref[j : j + 1, :]) * dot_tn(place[j], ret_out[...])
        mix = part if mix is None else mix + part
    layer[...] = (att[...].astype(F32) + mix).astype(BF16)
    stores = []

    def store(src, dst):
        copy = pltpu.make_async_copy(src, dst, local_sem.at[6 + len(stores)])
        copy.start()
        stores.append(copy)

    store(layer, layer_out)
    a1[1].wait_recv()
    b1[1].wait_recv()
    for number, (src, dst) in enumerate(((gv, gv_out), (gq, gq_out), (gk, gk_out))):
        for copies in last[number::3]:
            arrive(copies)
        store(src, dst)
    a2.wait_recv()
    gup[...] = (
        gw_own[2, rows_of(high, piece), :].astype(F32)
        + a1_recv[high].astype(F32)
        + a2_recv[...].astype(F32)
    )
    store(gup, gup_out)
    b2.wait_recv()
    gdown[...] = (
        gw_own[3, rows_of(low, piece), :].astype(F32)
        + b1_recv[low].astype(F32)
        + b2_recv[...].astype(F32)
    ).T
    store(gdown, gdown_out)
    for copy in sent:
        copy.wait_send()
    for copy in stores:
        copy.wait()


def copy_kernel(*refs):
    count = (len(refs) - 1) // 3
    sources, targets, held, sems = refs[:count], refs[count : 2 * count], refs[2 * count : -1], refs[-1]
    loads = [
        pltpu.make_async_copy(sources[n], held[n], sems.at[n]) for n in range(count)
    ]
    saves = [
        pltpu.make_async_copy(held[n], targets[n], sems.at[count + n]) for n in range(count)
    ]
    for load in loads:
        load.start()
    for load, save in zip(loads, saves):
        load.wait()
        save.start()
    for save in saves:
        save.wait()


def shards(
    query_input, key_input, value_input, routes, gate_values, up_weight, down_weight, cotangent
):
    rows, model = query_input.shape[1:]
    n_seq = lax.axis_size("seq")
    n_exp = lax.axis_size("expert")
    hidden = up_weight.shape[2]
    experts = up_weight.shape[0] * n_exp
    cap = rows * TOP * 3 // (2 * experts)
    cap = -(-cap // 16) * 16
    slots = experts * cap
    width = model // n_seq
    tokens = rows * n_seq
    half = model // 2
    piece = half // n_seq
    vmem = pl.BlockSpec(memory_space=pltpu.VMEM)
    hbm = pl.BlockSpec(memory_space=pl.ANY)
    dma = pltpu.SemaphoreType.DMA

    def shape(*dims, dtype=BF16):
        return jax.ShapeDtypeStruct(dims, dtype)

    def buf(*dims, dtype=BF16):
        return pltpu.VMEM(dims, dtype)

    head_block = buf(tokens, width)
    slot_block = buf(slots, model)
    row_block = buf(rows, model)
    out_shapes = [shape(rows, model)] * 4 + [
        shape(piece, hidden, dtype=F32),
        shape(hidden, piece, dtype=F32),
    ]
    results = pl.pallas_call(
        functools.partial(layer_kernel, experts, cap, 512),
        name="layer",
        out_shape=out_shapes,
        in_specs=[hbm] * 3 + [vmem] * 2 + [hbm] * 2 + [vmem],
        out_specs=[hbm] * 6,
        scratch_shapes=[
            row_block, row_block, row_block, row_block,
            buf(piece, hidden, dtype=F32),
            buf(hidden, piece, dtype=F32),
            head_block, head_block, head_block, head_block,
            buf(rows, model),
            buf(width // DH, tokens, tokens, dtype=F32),
            buf(width // DH, tokens, tokens),
            buf(rows, model),
            head_block, head_block, head_block, head_block,
            buf(TOP, slots, rows),
            slot_block, slot_block, slot_block, slot_block,
            slot_block, slot_block, slot_block, slot_block,
            buf(model, hidden),
            buf(hidden, model),
            buf(slots, hidden, dtype=F32),
            buf(slots, hidden),
            buf(slots, hidden),
            buf(model, slots),
            buf(model, slots),
            buf(4, 2 * piece, hidden),
            buf(4, 2 * piece, hidden),
            buf(4, 2 * piece, hidden),
            buf(2, piece, hidden),
            buf(2, piece, hidden),
            buf(piece, hidden), buf(piece, hidden), buf(piece, hidden), buf(piece, hidden),
            dma((5 + 3 * (width // DH), n_seq)),
            dma((5 + 3 * (width // DH), n_seq)),
            dma((4, n_exp)),
            dma((4, n_exp)),
            dma((4,)),
            dma((4,)),
            dma((6,)),
            dma((6,)),
            dma((12,)),
        ],
        compiler_params=pltpu.CompilerParams(
            collective_id=0, has_side_effects=True, vmem_limit_bytes=VMEM_LIMIT
        ),
        cost_estimate=pl.CostEstimate(
            flops=12 * slots * model * hidden, bytes_accessed=16 * model * hidden,
            transcendentals=0,
        ),
    )(
        query_input[0], key_input[0], value_input[0], routes[0].T, gate_values[0].T,
        up_weight[0], down_weight[0], cotangent[0],
    )
    results = pl.pallas_call(
        copy_kernel,
        name="outputs",
        out_shape=out_shapes,
        in_specs=[hbm] * 6,
        out_specs=[hbm] * 6,
        scratch_shapes=[pltpu.VMEM(out.shape, out.dtype) for out in out_shapes] + [dma((12,))],
        compiler_params=pltpu.CompilerParams(vmem_limit_bytes=VMEM_LIMIT),
    )(*results)
    return tuple(result[None] for result in results)


def solution(mesh):
    tokens = P(("dp", "expert"), "seq", None)
    weights = P("expert", None, None)
    in_specs = (tokens,) * 5 + (weights, weights, tokens)
    out_specs = (tokens,) * 4 + (P("expert", ("dp", "seq"), None), P("expert", None, ("dp", "seq")))
    return jax.shard_map(shards, mesh=mesh, in_specs=in_specs, out_specs=out_specs, check_vma=False)
```

```python
import functools
import math

import jax
import jax.numpy as jnp
from jax import lax
from jax.experimental import pallas as pl
from jax.experimental.pallas import tpu as pltpu
from jax.sharding import PartitionSpec as P

DH = 128
TOP = 2
EPSILON = 1e-06
GELU_COEF = math.sqrt(2.0 / math.pi)
MESH = pl.DeviceIdType.MESH
F32 = jnp.float32
BF16 = jnp.bfloat16
VMEM_LIMIT = 60 * 1024 * 1024


def gelu_pair(inputs):
    square = inputs * inputs
    hyper = jnp.tanh(inputs * (GELU_COEF + GELU_COEF * 0.044715 * square))
    half = 0.5 + 0.5 * hyper
    result = inputs * half
    slope = half + result * (1.0 - hyper) * (GELU_COEF + GELU_COEF * 3.0 * 0.044715 * square)
    return result, slope


def dot_nn(a, b):
    return jnp.dot(a, b, preferred_element_type=F32)


def dot_nt(a, b):
    return lax.dot_general(a, b, (((1,), (1,)), ((), ())), preferred_element_type=F32)


def dot_tn(a, b):
    return lax.dot_general(a, b, (((0,), (0,)), ((), ())), preferred_element_type=F32)


def greet(axes):
    barrier = pltpu.get_barrier_semaphore()
    total = 0
    for axis in axes:
        size = lax.axis_size(axis)
        me = lax.axis_index(axis)
        for step in range(1, size):
            peer = lax.rem(me + step, size)
            pl.semaphore_signal(barrier, inc=1, device_id={axis: peer}, device_id_type=MESH)
            total += 1
    pl.semaphore_wait(barrier, total)


def remote(src, dst, send, recv, axis, peer):
    return pltpu.make_async_remote_copy(
        src_ref=src,
        dst_ref=dst,
        send_sem=send,
        recv_sem=recv,
        device_id={axis: peer},
        device_id_type=MESH,
    )


def rows_of(index, count):
    return pl.ds(pl.multiple_of(index * count, count), count)


def split_cols(src, dst, send, recv, me, size, own_sem):
    rows = src.shape[0]
    width = src.shape[1] // size
    copies = []
    for step in range(1, size):
        peer = lax.rem(me + step, size)
        copy = remote(
            src.at[:, rows_of(peer, width)],
            dst.at[rows_of(me, rows), :],
            send.at[step],
            recv.at[step],
            "seq",
            peer,
        )
        copy.start()
        copies.append(copy)
    own = pltpu.make_async_copy(src.at[:, rows_of(me, width)], dst.at[rows_of(me, rows), :], own_sem)
    own.start()
    return copies, own


def join_block(src, dst, send, recv, me, size, step):
    rows = dst.shape[0]
    width = src.shape[1]
    peer = lax.rem(me + step, size)
    copy = remote(
        src.at[rows_of(peer, rows), :],
        dst.at[:, rows_of(me, width)],
        send.at[step],
        recv.at[step],
        "seq",
        peer,
    )
    copy.start()
    return copy


def swap_slots(src, dst, send, recv, me, size):
    cap = src.shape[0] // size
    copies = []
    for step in range(1, size):
        peer = lax.rem(me + step, size)
        copy = remote(
            src.at[rows_of(peer, cap), :],
            dst.at[rows_of(me, cap), :],
            send.at[step],
            recv.at[step],
            "expert",
            peer,
        )
        copy.start()
        copies.append(copy)
    dst[rows_of(me, cap), :] = src[rows_of(me, cap), :]
    return copies


def arrive(copies):
    for copy in copies:
        copy.wait_recv()


def softmax_rows(query, key):
    scores = dot_nt(query, key) * (1.0 / math.sqrt(DH))
    exponent = jnp.exp(scores - jnp.max(scores, axis=-1, keepdims=True))
    return exponent / jnp.sum(exponent, axis=-1, keepdims=True)


def as_column(row):
    size = row.shape[1]
    same = lax.broadcasted_iota(jnp.int32, (size, size), 0) == lax.broadcasted_iota(
        jnp.int32, (size, size), 1
    )
    return jnp.sum(jnp.where(same, row, 0.0), axis=1, keepdims=True)


def layer_kernel(
    experts, cap, chunk,
    q_hbm, k_hbm, v_hbm, routes_ref, gates_ref, up_hbm, down_hbm, cot_ref,
    layer_out, gq_out, gk_out, gv_out, gup_out, gdown_out,
    layer, gq, gk, gv, gup, gdown,
    qh, kh, vh, heads, att, probs, probs_t, datt, dheads, gqh, gkh, gvh,
    place, sent_grad, grad_in, sent_rows, rows_in, out_rows, dnorm_rows, ret_out, ret_dnorm,
    up, down, up_t, dact, act, dpre, rows_t, grad_t,
    gw_own, gw_other, gw_recv, a1_recv, b1_recv, a2_sent, a2_recv, b2_sent, b2_recv,
    seq_send, seq_recv, exp_send, exp_recv, dp_send, dp_recv, red_send, red_recv, local_sem,
):
    n_seq = lax.axis_size("seq")
    n_exp = lax.axis_size("expert")
    me_seq = lax.axis_index("seq")
    me_exp = lax.axis_index("expert")
    me_dp = lax.axis_index("dp")
    rows = cot_ref.shape[0]
    slots = experts * cap
    model, hidden = up.shape
    width = heads.shape[1]
    n_heads = width // DH
    sent = []

    load_down = pltpu.make_async_copy(down_hbm, down, local_sem.at[0])
    load_up = pltpu.make_async_copy(up_hbm, up, local_sem.at[1])
    greet(("seq", "expert", "dp"))

    seq_copies = []
    own_copies = []
    for number, (src, dst) in enumerate(((q_hbm, qh), (k_hbm, kh), (v_hbm, vh))):
        copies, own = split_cols(
            src, dst, seq_send.at[number], seq_recv.at[number], me_seq, n_seq,
            local_sem.at[2 + number],
        )
        seq_copies += copies
        own_copies.append(own)
    load_down.start()
    load_up.start()

    expert_ids = lax.broadcasted_iota(jnp.int32, (experts, rows), 0)
    hits = [
        jnp.where(routes_ref[j : j + 1, :] == expert_ids, 1.0, 0.0).astype(F32)
        for j in range(TOP)
    ]
    earlier = lax.broadcasted_iota(jnp.int32, (rows, rows), 0) < lax.broadcasted_iota(
        jnp.int32, (rows, rows), 1
    )
    rank = dot_nn(
        (hits[0] + hits[1]).astype(BF16), jnp.where(earlier, 1.0, 0.0).astype(BF16)
    )
    base = rank + (expert_ids * cap).astype(F32)
    slot_ids = lax.broadcasted_iota(jnp.int32, (slots, rows), 0).astype(F32)
    cot = cot_ref[...].astype(F32)
    gates = [as_column(gates_ref[j : j + 1, :]) for j in range(TOP)]
    packed = None
    for j in range(TOP):
        slot = jnp.sum(hits[j] * base, axis=0, keepdims=True)
        place[j] = jnp.where(slot_ids == slot, 1.0, 0.0).astype(BF16)
        part = dot_nn(place[j], (gates[j] * cot).astype(BF16))
        packed = part if packed is None else packed + part
    sent_grad[...] = packed.astype(BF16)
    grad_copies = swap_slots(sent_grad, grad_in, exp_send.at[0], exp_recv.at[0], me_exp, n_exp)
    sent += seq_copies + grad_copies

    for own in own_copies:
        own.wait()
    arrive(seq_copies)
    back = []
    for step in [*range(1, n_seq), 0]:
        block = rows_of(lax.rem(me_seq + step, n_seq), rows)
        for head in range(n_heads):
            cols = slice(head * DH, (head + 1) * DH)
            prob = softmax_rows(qh[block, cols], kh[:, cols])
            probs[head, block, :] = prob
            heads[block, cols] = dot_nn(prob.astype(BF16), vh[:, cols]).astype(BF16)
        if step > 0:
            back.append(
                join_block(heads, att, seq_send.at[3], seq_recv.at[3], me_seq, n_seq, step)
            )
        else:
            att[:, rows_of(me_seq, width)] = heads[block, :]
    arrive(back)
    sent += back

    att_f = att[...].astype(F32)
    inverse = lax.rsqrt(jnp.mean(att_f * att_f, axis=-1, keepdims=True) + EPSILON)
    placer = place[0] + place[1]
    sent_rows[...] = dot_nn(placer, (att_f * inverse).astype(BF16)).astype(BF16)
    row_copies = swap_slots(sent_rows, rows_in, exp_send.at[1], exp_recv.at[1], me_exp, n_exp)
    sent += row_copies
    for head in range(n_heads):
        probs_t[head] = probs[head].astype(BF16).T
    arrive(grad_copies)
    load_down.wait()
    load_up.wait()

    @pl.loop(0, hidden // chunk)
    def _(c):
        cols = rows_of(c, chunk)
        dact[:, cols] = dot_nt(grad_in[...], down[cols, :])

    grad_t[...] = grad_in[...].T

    @pl.loop(0, model // 256)
    def _(c):
        cols = rows_of(c, 256)
        up_t[:, cols] = up[cols, :].T

    arrive(row_copies)

    for c in range(hidden // chunk):
        cols = slice(c * chunk, (c + 1) * chunk)
        value, slope = gelu_pair(dot_nn(rows_in[...], up[:, cols]))
        act[:, cols] = value.astype(BF16)
        dpre[:, cols] = (dact[:, cols] * slope).astype(BF16)

    half = model // 2
    piece = half // n_seq
    pair = 2 * piece
    low = lax.rem(me_seq, 2)
    high = me_seq // 2
    peer_low = 2 * high + 1 - low
    peer_high = 2 * (1 - high) + low

    def grads_first(dst, core, bit):
        left = jnp.concatenate(
            [rows_t[rows_of(core * n_seq + 2 * n + bit, piece), :] for n in range(2)], axis=0
        )

        @pl.loop(0, hidden // chunk)
        def _(c):
            cols = rows_of(c, chunk)
            dst[:, cols] = dot_nn(left, dpre[:, cols]).astype(BF16)

    def grads_second(dst, core, bit):
        left = grad_t[rows_of(core * (n_seq // 2) + bit, pair), :]

        @pl.loop(0, hidden // chunk)
        def _(c):
            cols = rows_of(c, chunk)
            dst[:, cols] = dot_nn(left, act[:, cols]).astype(BF16)

    def core_send(number):
        copy = remote(
            gw_other.at[number], gw_recv.at[number], dp_send.at[number], dp_recv.at[number],
            "dp", 1 - me_dp,
        )
        copy.start()
        sent.append(copy)
        return copy

    def add_core(number):
        @pl.loop(0, hidden // chunk)
        def _(c):
            cols = rows_of(c, chunk)
            gw_own[number, :, cols] = (
                gw_own[number, :, cols].astype(F32) + gw_recv[number, :, cols].astype(F32)
            ).astype(BF16)

    def reduce_send(src, dst, number, peer):
        copy = remote(src, dst, red_send.at[number], red_recv.at[number], "seq", peer)
        copy.start()
        sent.append(copy)
        return copy

    grads_second(gw_other.at[1], 1 - me_dp, 1 - high)
    core_second = core_send(1)
    rows_t[...] = rows_in[...].T
    grads_first(gw_other.at[0], 1 - me_dp, 1 - low)
    core_first = core_send(0)
    grads_second(gw_own.at[1], me_dp, 1 - high)
    grads_first(gw_own.at[0], me_dp, 1 - low)

    @pl.loop(0, model // 256)
    def _(c):
        cols = rows_of(c, 256)
        dnorm_rows[:, cols] = dot_nn(dpre[...], up_t[:, cols]).astype(BF16)

    dnorm_copies = swap_slots(
        dnorm_rows, ret_dnorm, exp_send.at[2], exp_recv.at[2], me_exp, n_exp
    )
    sent += dnorm_copies

    core_second.wait_recv()
    add_core(1)
    b1 = []
    for number, which in enumerate((1 - low, low), 2):
        b1.append(
            reduce_send(
                gw_own.at[1, rows_of(which, piece), :], b1_recv.at[which], number, peer_high
            )
        )
    core_first.wait_recv()
    add_core(0)
    a1 = []
    for number, which in enumerate((1 - high, high)):
        a1.append(
            reduce_send(gw_own.at[0, rows_of(which, piece), :], a1_recv.at[which], number, peer_low)
        )

    grads_first(gw_other.at[2], 1 - me_dp, low)
    core_third = core_send(2)
    grads_second(gw_other.at[3], 1 - me_dp, high)
    core_fourth = core_send(3)
    grads_first(gw_own.at[2], me_dp, low)
    grads_second(gw_own.at[3], me_dp, high)

    @pl.loop(0, model // 256)
    def _(c):
        cols = rows_of(c, 256)
        out_rows[:, cols] = dot_nn(act[...], down[:, cols]).astype(BF16)

    core_third.wait_recv()
    add_core(2)
    core_fourth.wait_recv()
    add_core(3)

    def join_head(src, dst, head, number):
        cols = slice(head * DH, (head + 1) * DH)
        there = pl.ds(pl.multiple_of(me_seq * width + head * DH, DH), DH)
        copies = []
        for step in range(1, n_seq):
            peer = lax.rem(me_seq + step, n_seq)
            copy = remote(
                src.at[rows_of(peer, rows), cols],
                dst.at[:, there],
                seq_send.at[number, step],
                seq_recv.at[number, step],
                "seq",
                peer,
            )
            copy.start()
            copies.append(copy)
        dst[:, there] = src[rows_of(me_seq, rows), cols]
        return copies

    arrive(dnorm_copies)
    out_copies = swap_slots(out_rows, ret_out, exp_send.at[3], exp_recv.at[3], me_exp, n_exp)
    sent += out_copies
    dunit = dot_tn(place[0] + place[1], ret_dnorm[...])
    att_f = att[...].astype(F32)
    inverse = lax.rsqrt(jnp.mean(att_f * att_f, axis=-1, keepdims=True) + EPSILON)
    unit = att_f * inverse
    datt[...] = (
        cot_ref[...].astype(F32)
        + inverse * (dunit - unit * jnp.mean(dunit * unit, axis=-1, keepdims=True))
    ).astype(BF16)
    datt_copies, own = split_cols(
        datt, dheads, seq_send.at[4], seq_recv.at[4], me_seq, n_seq, local_sem.at[5]
    )
    sent += datt_copies
    own.wait()
    arrive(datt_copies)

    scaling = 1.0 / math.sqrt(DH)
    last = []
    for head in range(n_heads):
        cols = slice(head * DH, (head + 1) * DH)
        prob = probs[head]
        dhead = dheads[:, cols]
        dprobs = dot_nt(dhead, vh[:, cols])
        gvh[:, cols] = dot_nn(probs_t[head], dhead).astype(BF16)
        last.append(join_head(gvh, gv, head, 5 + 3 * head))
        delta = jnp.sum(prob * dprobs, axis=-1, keepdims=True)
        dscores = (prob * (dprobs - delta) * scaling).astype(BF16)
        gqh[:, cols] = dot_nn(dscores, kh[:, cols]).astype(BF16)
        last.append(join_head(gqh, gq, head, 6 + 3 * head))
        gkh[:, cols] = dot_tn(dscores, qh[:, cols]).astype(BF16)
        last.append(join_head(gkh, gk, head, 7 + 3 * head))
        if head == 0:
            a1[0].wait_recv()
            a2_sent[...] = (
                gw_own[2, rows_of(1 - high, piece), :].astype(F32)
                + a1_recv[1 - high].astype(F32)
            ).astype(BF16)
            a2 = reduce_send(a2_sent, a2_recv, 4, peer_high)
            b1[0].wait_recv()
            b2_sent[...] = (
                gw_own[3, rows_of(1 - low, piece), :].astype(F32)
                + b1_recv[1 - low].astype(F32)
            ).astype(BF16)
            b2 = reduce_send(b2_sent, b2_recv, 5, peer_low)
    for copies in last:
        sent += copies

    arrive(out_copies)
    mix = None
    for j in range(TOP):
        part = as_column(gates_ref[j : j + 1, :]) * dot_tn(place[j], ret_out[...])
        mix = part if mix is None else mix + part
    layer[...] = (att[...].astype(F32) + mix).astype(BF16)
    stores = []

    def store(src, dst):
        copy = pltpu.make_async_copy(src, dst, local_sem.at[6 + len(stores)])
        copy.start()
        stores.append(copy)

    store(layer, layer_out)
    a1[1].wait_recv()
    b1[1].wait_recv()
    for number, (src, dst) in enumerate(((gv, gv_out), (gq, gq_out), (gk, gk_out))):
        for copies in last[number::3]:
            arrive(copies)
        store(src, dst)
    a2.wait_recv()
    gup[...] = (
        gw_own[2, rows_of(high, piece), :].astype(F32)
        + a1_recv[high].astype(F32)
        + a2_recv[...].astype(F32)
    )
    store(gup, gup_out)
    b2.wait_recv()
    gdown[...] = (
        gw_own[3, rows_of(low, piece), :].astype(F32)
        + b1_recv[low].astype(F32)
        + b2_recv[...].astype(F32)
    ).T
    store(gdown, gdown_out)
    for copy in sent:
        copy.wait_send()
    for copy in stores:
        copy.wait()


def copy_kernel(*refs):
    count = (len(refs) - 1) // 3
    sources, targets, held, sems = refs[:count], refs[count : 2 * count], refs[2 * count : -1], refs[-1]
    loads = [
        pltpu.make_async_copy(sources[n], held[n], sems.at[n]) for n in range(count)
    ]
    saves = [
        pltpu.make_async_copy(held[n], targets[n], sems.at[count + n]) for n in range(count)
    ]
    for load in loads:
        load.start()
    for load, save in zip(loads, saves):
        load.wait()
        save.start()
    for save in saves:
        save.wait()


def shards(
    query_input, key_input, value_input, routes, gate_values, up_weight, down_weight, cotangent
):
    rows, model = query_input.shape[1:]
    n_seq = lax.axis_size("seq")
    n_exp = lax.axis_size("expert")
    hidden = up_weight.shape[2]
    experts = up_weight.shape[0] * n_exp
    cap = rows * TOP * 3 // (2 * experts)
    cap = -(-cap // 16) * 16
    slots = experts * cap
    width = model // n_seq
    tokens = rows * n_seq
    half = model // 2
    piece = half // n_seq
    vmem = pl.BlockSpec(memory_space=pltpu.VMEM)
    hbm = pl.BlockSpec(memory_space=pl.ANY)
    dma = pltpu.SemaphoreType.DMA

    def shape(*dims, dtype=BF16):
        return jax.ShapeDtypeStruct(dims, dtype)

    def buf(*dims, dtype=BF16):
        return pltpu.VMEM(dims, dtype)

    head_block = buf(tokens, width)
    slot_block = buf(slots, model)
    row_block = buf(rows, model)
    out_shapes = [shape(rows, model)] * 4 + [
        shape(piece, hidden, dtype=F32),
        shape(hidden, piece, dtype=F32),
    ]
    results = pl.pallas_call(
        functools.partial(layer_kernel, experts, cap, 512),
        name="layer",
        out_shape=out_shapes,
        in_specs=[hbm] * 3 + [vmem] * 2 + [hbm] * 2 + [vmem],
        out_specs=[hbm] * 6,
        scratch_shapes=[
            row_block, row_block, row_block, row_block,
            buf(piece, hidden, dtype=F32),
            buf(hidden, piece, dtype=F32),
            head_block, head_block, head_block, head_block,
            buf(rows, model),
            buf(width // DH, tokens, tokens, dtype=F32),
            buf(width // DH, tokens, tokens),
            buf(rows, model),
            head_block, head_block, head_block, head_block,
            buf(TOP, slots, rows),
            slot_block, slot_block, slot_block, slot_block,
            slot_block, slot_block, slot_block, slot_block,
            buf(model, hidden),
            buf(hidden, model),
            buf(hidden, model),
            buf(slots, hidden, dtype=F32),
            buf(slots, hidden),
            buf(slots, hidden),
            buf(model, slots),
            buf(model, slots),
            buf(4, 2 * piece, hidden),
            buf(4, 2 * piece, hidden),
            buf(4, 2 * piece, hidden),
            buf(2, piece, hidden),
            buf(2, piece, hidden),
            buf(piece, hidden), buf(piece, hidden), buf(piece, hidden), buf(piece, hidden),
            dma((5 + 3 * (width // DH), n_seq)),
            dma((5 + 3 * (width // DH), n_seq)),
            dma((4, n_exp)),
            dma((4, n_exp)),
            dma((4,)),
            dma((4,)),
            dma((6,)),
            dma((6,)),
            dma((12,)),
        ],
        compiler_params=pltpu.CompilerParams(
            collective_id=0, has_side_effects=True, vmem_limit_bytes=VMEM_LIMIT
        ),
        cost_estimate=pl.CostEstimate(
            flops=12 * slots * model * hidden, bytes_accessed=16 * model * hidden,
            transcendentals=0,
        ),
    )(
        query_input[0], key_input[0], value_input[0], routes[0].T, gate_values[0].T,
        up_weight[0], down_weight[0], cotangent[0],
    )
    results = pl.pallas_call(
        copy_kernel,
        name="outputs",
        out_shape=out_shapes,
        in_specs=[hbm] * 6,
        out_specs=[hbm] * 6,
        scratch_shapes=[pltpu.VMEM(out.shape, out.dtype) for out in out_shapes] + [dma((12,))],
        compiler_params=pltpu.CompilerParams(vmem_limit_bytes=VMEM_LIMIT),
    )(*results)
    return tuple(result[None] for result in results)


def solution(mesh):
    tokens = P(("dp", "expert"), "seq", None)
    weights = P("expert", None, None)
    in_specs = (tokens,) * 5 + (weights, weights, tokens)
    out_specs = (tokens,) * 4 + (P("expert", ("dp", "seq"), None), P("expert", None, ("dp", "seq")))
    return jax.shard_map(shards, mesh=mesh, in_specs=in_specs, out_specs=out_specs, check_vma=False)
```
